256 devices in a mesh: wide: 64 (over x, y, z_lo, core), narrow: 4 (over z_hi).
Axes of the slice: x: 4, y: 4, z: 8 (z_hi: 4, z_lo: 2; z = z_hi * 2 + z_lo), core: 2. Of those that a mesh axis runs over, the one named last changes fastest.
Arguments:
- raster: int32 [512, 8192], P('narrow', 'wide'), may hold values from 0 to 1
- transmission: bfloat16 [512, 8192], P('narrow', 'wide'), may hold values from 0.5 to 1.5
- kernels: float32 [8, 2, 64, 64], replicated, may hold values from -0.09375 to 0.09375
- kernel_weight: float32 [8], replicated, may hold values from 0.1 to 1
- library: bfloat16 [524288, 256], P(('wide', 'narrow')), may hold values from -40 to 40
- clip_tile: int32 [1024], replicated, may hold values from 0 to 255, as said below
- clip_corner: int32 [2, 1024], replicated, may hold values from 0 to 64
Outputs:
- aerial: float32 [512, 8192], P('narrow', 'wide')
- scores: float32 [1024], P(('wide', 'narrow'))
The draws below stay inside these ranges and needn't reach their ends.
Inputs may be any that keep to these rules, and one draw needn't show every extreme that they name: `clip_tile`: each tile owns at most 16 clips, and some tile owns exactly 16.
All inputs are finite; a program needn't handle non-finite values.
Results may differ from the reference program's by a relative error of at most 0.0011.
Values may be sent and summed in bfloat16 or wider, within the bound.
A program may use at most 64 MiB of HBM per device.

```python
import math
import jax
import jax.numpy as jnp
from jax import lax

TILE = 128
KERNELS = 8
KSIZE = 64
CLIP = 64
KSIG = 16
LIB_DEV = 2048
CAP = 16
SIGD = 256
GRID_COLS = 64
TILES = 256
NX = 512
NY = 8192
CLIPS = 1024
LIB = 524288


def clip_owners(key):
    key_hot, key_order, key_shuffle = jax.random.split(jax.random.fold_in(key, 11), 3)
    slot_count = TILES * CAP
    busiest = jax.random.randint(key_hot, (), 0, TILES)
    slot_owner = jnp.arange(slot_count, dtype=jnp.int32) // CAP
    ranking = jax.random.permutation(key_order, slot_count).astype(jnp.int32)
    priority = jnp.where(slot_owner == busiest, -1, ranking)
    chosen = jnp.argsort(priority, stable=True)[:CLIPS]
    chosen = chosen[jax.random.permutation(key_shuffle, CLIPS)]
    return (chosen // CAP).astype(jnp.int32)


def layout_draws(key):
    key_raster, key_light, key_taps, key_weight, key_corner = jax.random.split(jax.random.fold_in(key, 5), 5)
    raster = jax.random.randint(key_raster, (NX, NY), 0, 2, dtype=jnp.int32)
    transmission = jax.random.uniform(key_light, (NX, NY), jnp.float32, 0.5, 1.5).astype(jnp.bfloat16)
    kernels = jnp.clip(jax.random.normal(key_taps, (KERNELS, 2, KSIZE, KSIZE), jnp.float32), -4.0, 4.0) * (math.sqrt(2.0) / KSIZE)
    log_weight = jax.random.uniform(key_weight, (KERNELS,), jnp.float32, math.log(0.1), 0.0)
    kernel_weight = jnp.clip(jnp.exp(log_weight), 0.1, 1.0)
    clip_corner = jax.random.randint(key_corner, (2, CLIPS), 0, TILE - CLIP + 1, dtype=jnp.int32)
    return (raster, transmission, kernels, kernel_weight, clip_corner)


def dct_table():
    freq_index = jnp.arange(KSIG, dtype=jnp.float32)[:, None]
    pixel_index = jnp.arange(CLIP, dtype=jnp.float32)[None, :]
    weights = jnp.where(freq_index == 0, jnp.sqrt(jnp.float32(1.0 / CLIP)), jnp.sqrt(jnp.float32(2.0 / CLIP)))
    return weights * jnp.cos(jnp.pi * (pixel_index + 0.5) * freq_index / CLIP)


def complex_product(formula, left_real, left_imag, right_real, right_imag):
    highest = lax.Precision.HIGHEST

    def single(left_operand, right_operand):
        return jnp.einsum(formula, left_operand, right_operand, precision=highest)
    real_part = single(left_real, right_real) - single(left_imag, right_imag)
    imag_part = single(left_real, right_imag) + single(left_imag, right_real)
    return (real_part, imag_part)


def drawn_units(key, planted_count):
    raster, transmission, kernels, kernel_weight, clip_corner = layout_draws(key)
    clip_tile = clip_owners(key)
    highest = lax.Precision.HIGHEST
    half_width = KSIZE // 2
    mask_values = raster.astype(jnp.float32) * transmission.astype(jnp.float32)
    padded = jnp.pad(mask_values, ((half_width, half_width), (half_width, half_width)))
    patch_size = CLIP + KSIZE
    grid_index = jnp.arange(patch_size, dtype=jnp.int32)
    phase_angle = 2.0 * math.pi / patch_size * jnp.mod(grid_index[:, None] * grid_index[None, :], patch_size).astype(jnp.float32)
    cosine_table = jnp.cos(phase_angle)
    sine_table = jnp.sin(phase_angle)
    taps_cos = cosine_table[:, :KSIZE]
    taps_sin = sine_table[:, :KSIZE]
    section_real, section_imag = complex_product('ai,kij->kaj', taps_cos, taps_sin, kernels[:, 0], kernels[:, 1])
    gain_real, gain_imag = complex_product('kaj,bj->kab', section_real, section_imag, taps_cos, taps_sin)
    out_cos = cosine_table[:CLIP]
    out_sin = sine_table[:CLIP]
    dct_rows = dct_table()
    keep_mask = (jnp.arange(SIGD, dtype=jnp.int32) != 0).astype(jnp.float32)
    picked = jax.random.permutation(jax.random.fold_in(key, 29), CLIPS)[:planted_count]
    row_first = (clip_tile // GRID_COLS * TILE + clip_corner[0])[picked].astype(jnp.int32)
    col_first = (clip_tile % GRID_COLS * TILE + clip_corner[1])[picked].astype(jnp.int32)
    scale_factor = 1.0 / (patch_size * patch_size)

    def one_clip(corner_pair):
        patch_cells = lax.dynamic_slice(padded, (corner_pair[0], corner_pair[1]), (patch_size, patch_size))
        half_real = jnp.dot(cosine_table, patch_cells, precision=highest)
        half_imag = -jnp.dot(sine_table, patch_cells, precision=highest)
        spec_real = jnp.dot(half_real, cosine_table, precision=highest) + jnp.dot(half_imag, sine_table, precision=highest)
        spec_imag = jnp.dot(half_imag, cosine_table, precision=highest) - jnp.dot(half_real, sine_table, precision=highest)
        filt_real = spec_real[None] * gain_real - spec_imag[None] * gain_imag
        filt_imag = spec_real[None] * gain_imag + spec_imag[None] * gain_real
        left_real, left_imag = complex_product('xa,kab->kxb', out_cos, out_sin, filt_real, filt_imag)
        field_real, field_imag = complex_product('kxb,yb->kxy', left_real, left_imag, out_cos, out_sin)
        energy = (field_real * scale_factor) ** 2 + (field_imag * scale_factor) ** 2
        window = jnp.einsum('k,kxy->xy', kernel_weight, energy, precision=highest)
        halfway = jnp.dot(dct_rows, window, precision=highest)
        signature = jnp.dot(halfway, dct_rows.T, precision=highest).reshape(SIGD) * keep_mask
        return signature / jnp.sqrt(jnp.sum(signature * signature) + 1e-12)
    return lax.map(one_clip, jnp.stack([row_first, col_first], axis=1))


def draw_raster(key, part):
    return layout_draws(key)[0]


def draw_transmission(key, part):
    return layout_draws(key)[1]


def draw_kernels(key, part):
    return layout_draws(key)[2]


def draw_kernel_weight(key, part):
    return layout_draws(key)[3]


def draw_clip_corner(key, part):
    return layout_draws(key)[4]


def draw_clip_tile(key, part):
    return clip_owners(key)


def draw_library(key, part):
    planted_count = CLIPS // 4
    clip_units = drawn_units(key, planted_count)
    key_list = jax.random.split(jax.random.fold_in(key, 23), 9)
    magnitude = jnp.exp(jax.random.uniform(key_list[0], (LIB, 1), jnp.float32, math.log(4.0), math.log(40.0)))
    sign_flip = (2 * jax.random.randint(key_list[1], (LIB, 1), 0, 2) - 1).astype(jnp.float32)
    column = jnp.arange(SIGD, dtype=jnp.int32)[None, :]
    noise_part = jnp.clip(jax.random.normal(key_list[3], (LIB, SIGD), jnp.float32), -4.0, 4.0) * 0.05
    background = jnp.where(column == 0, jnp.minimum(magnitude, 40.0) * sign_flip, noise_part)
    near_ratio = jnp.exp(jax.random.uniform(key_list[4], (planted_count, 1), jnp.float32, math.log(0.02), math.log(0.25)))
    far_ratio = jnp.sqrt(near_ratio * near_ratio + jax.random.uniform(key_list[5], (planted_count, 1), jnp.float32, 1.0, 3.0) / 200.0)
    ratios = jnp.stack([near_ratio, far_ratio])
    directions = jax.random.normal(key_list[6], (2, planted_count, SIGD), jnp.float32)
    directions = directions - jnp.sum(directions * clip_units[None], axis=2, keepdims=True) * clip_units[None]
    directions = directions / jnp.sqrt(jnp.sum(directions * directions, axis=2, keepdims=True))
    amplitude = jnp.exp(jax.random.uniform(key_list[7], (2, planted_count, 1), jnp.float32, math.log(0.5), math.log(4.0)))
    copies = (amplitude * (clip_units[None] + ratios * directions)).reshape(2 * planted_count, SIGD)
    positions = jax.random.permutation(key_list[8], LIB)[:2 * planted_count]
    library_rows = background.at[positions].set(copies)
    return library_rows.astype(jnp.bfloat16)


def setup_inputs(seed: int = 0) -> dict:
    key_of = jax.random.split(jax.random.key(seed), 8)
    return {
        "raster": draw_raster(jax.random.fold_in(key_of[7], 71), 0),
        "transmission": draw_transmission(jax.random.fold_in(key_of[7], 71), 0),
        "kernels": draw_kernels(jax.random.fold_in(key_of[7], 71), 0),
        "kernel_weight": draw_kernel_weight(jax.random.fold_in(key_of[7], 71), 0),
        "library": draw_library(jax.random.fold_in(key_of[7], 71), 0),
        "clip_tile": draw_clip_tile(jax.random.fold_in(key_of[7], 71), 0),
        "clip_corner": draw_clip_corner(jax.random.fold_in(key_of[7], 71), 0),
    }


sharpness = 400.0

def dct_basis():
    freq_index = jnp.arange(KSIG, dtype=jnp.float32)[:, None]
    pixel_index = jnp.arange(CLIP, dtype=jnp.float32)[None, :]
    weights = jnp.where(freq_index == 0, jnp.sqrt(jnp.float32(1.0 / CLIP)), jnp.sqrt(jnp.float32(2.0 / CLIP)))
    return weights * jnp.cos(jnp.pi * (pixel_index + 0.5) * freq_index / CLIP)

def normalize(matrix):
    mean_square = lax.optimization_barrier(jnp.mean(matrix * matrix, axis=1, keepdims=True))
    return (matrix / (KSIG * jnp.sqrt(mean_square + 1e-06))).astype(jnp.bfloat16)

def reference(raster, transmission, kernels, kernel_weight, library, clip_tile, clip_corner):
    mask_values = raster.astype(jnp.float32) * transmission.astype(jnp.float32)
    half_width = KSIZE // 2
    padded = jnp.pad(mask_values, ((half_width, half_width), (half_width, half_width)))
    spectrum = jnp.fft.fft2(padded)
    aerial = jnp.zeros((NX, NY), jnp.float32)
    for kernel_index in range(KERNELS):
        conj_taps = kernels[kernel_index, 0] - 1j * kernels[kernel_index, 1]
        spread = jnp.zeros(padded.shape, spectrum.dtype)
        spread = spread.at[:KSIZE, :KSIZE].set(conj_taps.astype(spectrum.dtype))
        tile_field = jnp.fft.ifft2(spectrum * jnp.conj(jnp.fft.fft2(spread)))[:NX, :NY]
        aerial = aerial + kernel_weight[kernel_index] * (jnp.real(tile_field) ** 2 + jnp.imag(tile_field) ** 2)
    grid_row = clip_tile // GRID_COLS
    grid_col = clip_tile % GRID_COLS
    row_start = (grid_row * TILE + clip_corner[0]).astype(jnp.int32)
    col_start = (grid_col * TILE + clip_corner[1]).astype(jnp.int32)

    def window(row_first, col_first):
        return lax.dynamic_slice(aerial, (row_first, col_first), (CLIP, CLIP))
    windows = jax.vmap(window)(row_start, col_start)
    dct_rows = dct_basis()
    halfway = jnp.einsum('ku,cuv->ckv', dct_rows, windows, precision=lax.Precision.HIGHEST)
    signature = jnp.einsum('ckv,lv->ckl', halfway, dct_rows, precision=lax.Precision.HIGHEST).reshape(CLIPS, SIGD)
    signature = jnp.where(jnp.arange(SIGD)[None, :] == 0, 0.0, signature)
    clip_units = normalize(signature)
    blocks = library.reshape(TILES, LIB_DEV, SIGD)

    def absorb(running, lib_block):
        peak_old, total_old = running
        lib_units = normalize(lib_block.astype(jnp.float32))
        logits = sharpness * (jnp.dot(clip_units, lib_units.T, preferred_element_type=jnp.float32) - 1.0)
        peak_new = jnp.maximum(peak_old, lax.optimization_barrier(jnp.max(logits, axis=1)))
        total_new = total_old * jnp.exp(peak_old - peak_new) + lax.optimization_barrier(jnp.sum(jnp.exp(logits - peak_new[:, None]), axis=1))
        return ((peak_new, total_new), None)
    start_pair = (jnp.full((CLIPS,), -1e+30, jnp.float32), jnp.zeros((CLIPS,), jnp.float32))
    (peak_all, total_sum), unused = lax.scan(absorb, start_pair, blocks)
    scores = -(peak_all + jnp.log(total_sum)) / sharpness
    return (aerial, scores)
```

```python
import math

import jax
import jax.numpy as jnp
from jax import lax
from jax.experimental import pallas as pl
from jax.experimental.pallas import tpu as pltpu
from jax.sharding import PartitionSpec as P

TILE = 128
TAPS = 64
HALF = 32
KSIG = 16
CAP = 16
SIGD = 256
FIELDS = 16
SHIFTS = 16
DEPTH = 5 * 1024
GROUPS = 16
OWN_IDS = 512
CLIPS = 1024
LIB_DEV = 2048
SHARP = 400.0
F32 = jnp.float32
BF16 = jnp.bfloat16
I32 = jnp.int32
MESH = pl.DeviceIdType.MESH
HIGHEST = lax.Precision.HIGHEST

PLANE = sorted(
    [(dx, dy) for dx in range(4) for dy in range(4) if dx or dy],
    key=lambda d: -(min(d[0], 4 - d[0]) + min(d[1], 4 - d[1])),
)
LINE = sorted(
    [(dz, dc) for dz in range(8) for dc in range(2) if dz or dc],
    key=lambda d: -(2 * min(d[0], 8 - d[0]) + d[1]),
)
RING = sorted(range(1, 8), key=lambda d: -min(d, 8 - d))
AROUND = [(dw, dn) for dw in (1, -1, 0) for dn in (1, -1, 0) if dw or dn]


def place():
    w = lax.axis_index("wide")
    n = lax.axis_index("narrow")
    return w, n


def plane_peer(w, n, d):
    g = w // 4
    x = (g // 4 + d[0]) % 4
    y = (g % 4 + d[1]) % 4
    return (x * 4 + y) * 4 + w % 4, n


def line_peer(w, n, d):
    z = (n * 2 + (w // 2) % 2 + d[0]) % 8
    c = (w % 2 + d[1]) % 2
    return (w // 4) * 4 + (z % 2) * 2 + c, z // 2


def around_peer(w, n, d):
    return (w + d[0] + 64) % 64, (n + d[1] + 4) % 4


def iota(shape, dim):
    return lax.broadcasted_iota(I32, shape, dim)


def dot(a, b, precision=None):
    return jnp.dot(a, b, preferred_element_type=F32, precision=precision)


def dot_nt(a, b, precision=None):
    return lax.dot_general(
        a, b, (((1,), (1,)), ((), ())), preferred_element_type=F32, precision=precision
    )


def wait_bytes(ref, sem):
    pltpu.make_async_copy(ref, ref, sem).wait()


def unit_rows(matrix):
    mean_square = jnp.mean(matrix * matrix, axis=1, keepdims=True)
    return (matrix / (KSIG * jnp.sqrt(mean_square + 1e-06))).astype(BF16)


def build_taps(kern_ref, raw_taps, perm, taps):
    for block in range(8):
        p = iota((128, 1024), 0) + block * 128
        q = iota((128, 1024), 1)
        hit = q == (p % 64) * 16 + p // 64
        perm[block * 128 : block * 128 + 128, :] = jnp.where(hit, 1.0, 0.0).astype(BF16)
    for i in range(0, TAPS, 2):
        pair = jnp.concatenate(
            [kern_ref[pl.ds(i, 16, stride=64), :], kern_ref[pl.ds(i + 1, 16, stride=64), :]],
            axis=1,
        )
        high = pair.astype(BF16)
        low = (pair - high.astype(F32)).astype(BF16)
        row = (i // 16) * 32
        lane = (i % 16) * 64
        raw_taps[row : row + 16, lane : lane + 128] = high
        raw_taps[row + 16 : row + 32, lane : lane + 128] = low
    raw_taps[...] = dot(raw_taps[...], perm[...]).astype(BF16)

    def shift(s, carry):
        inner = iota((32, 128), 1) % 16
        wrap = inner >= 16 - s
        row = pl.multiple_of(s * 16, 16)
        for v in range(8):
            lanes = slice(v * 128, v * 128 + 128)
            for ib in range(5):
                zero = jnp.zeros((32, 128), BF16)
                here = raw_taps[ib * 32 : ib * 32 + 32, lanes] if ib < 4 else zero
                if ib > 0:
                    last = pltpu.roll(raw_taps[ib * 32 - 32 : ib * 32, lanes], 112, 1)
                else:
                    last = zero
                moved = pltpu.roll(jnp.where(wrap, last, here), s, 1)
                to = slice(ib * 1024 + v * 128, ib * 1024 + v * 128 + 128)
                taps[pl.ds(row, 16), to] = moved[0:16]
                taps[pl.ds(row + 256, 16), to] = moved[16:32]
        return carry

    lax.fori_loop(0, SHIFTS, shift, 0)


def cosine(m):
    v = (64 - jnp.abs(m - 128)).astype(F32) * (math.pi / 128)
    s = v * v
    poly = 1.0 / 6227020800.0
    for c in (-1.0 / 39916800, 1.0 / 362880, -1.0 / 5040, 1.0 / 120, -1.0 / 6, 1.0):
        poly = poly * s + c
    return -(v * poly)


def shifted_basis(corner):
    spread = (iota((256, 16), 0) // 16 == iota((256, 16), 1)).astype(F32)
    corners = dot(spread, jnp.broadcast_to(corner, (16, 128))).astype(I32)
    k = iota((256, 128), 0) % 16
    offset = iota((256, 128), 1) - corners
    inside = (offset >= 0) & (offset < 64)
    weight = jnp.where(k == 0, math.sqrt(1.0 / 64), math.sqrt(2.0 / 64)).astype(F32)
    m = jnp.where(inside, ((2 * offset + 1) * k) % 256, 0)
    return jnp.where(inside, weight * cosine(m), 0.0)


def own_bases(w, n, tile_ref, corner_ref, row_basis, col_basis):
    owned = (tile_ref[...] == n * 64 + w).astype(F32)
    earlier = (iota((128, 128), 0) < iota((128, 128), 1)).astype(F32)
    before = dot(owned, earlier)
    base = jnp.zeros((1, 1), F32)
    slot = iota((16, 128), 0).astype(F32)
    rows = jnp.zeros((16, 128), F32)
    cols = jnp.zeros((16, 128), F32)
    for r in range(8):
        own = owned[r : r + 1]
        here = (own > 0) & (before[r : r + 1] + base == slot)
        part = slice(r * 128, r * 128 + 128)
        rows += jnp.where(here, corner_ref[0:1, part].astype(F32), 0.0)
        cols += jnp.where(here, corner_ref[1:2, part].astype(F32), 0.0)
        base += jnp.sum(own, axis=1, keepdims=True)
    row_basis[...] = shifted_basis(jnp.sum(rows, axis=1, keepdims=True))
    col_basis[...] = shifted_basis(jnp.sum(cols, axis=1, keepdims=True))


def build_select(w, tile_ref, select):
    core = w % 2
    q = iota((64, 256), 1)
    dev = q // 16
    slot_key = ((dev % 4) * 64 + (w // 4) * 4 + dev // 4) * 16 + q % 16
    for r in range(8):
        m = iota((64, 128), 0) + r * 64
        ids = (m // 16) * 32 + core * 16 + m % 16
        lane = iota((64, 128), 1)
        tiles = tile_ref[r : r + 1, :]
        mine = jnp.sum(
            jnp.where(ids == lane + r * 128, tiles.astype(F32), 0.0), axis=1, keepdims=True
        )
        rank = jnp.zeros((64, 128), F32)
        for b in range(r + 1):
            same = tile_ref[b : b + 1, :].astype(F32) == mine
            if b == r:
                same = same & (lane + r * 128 < ids)
            rank += jnp.where(same, 1.0, 0.0)
        key = (mine * 16.0 + jnp.sum(rank, axis=1, keepdims=True)).astype(I32)
        select[r * 64 : r * 64 + 64, :] = (key == slot_key).astype(F32).astype(BF16)


def shifted_copies(ext, spread):
    lane = iota((192, 128), 1)
    left = pltpu.roll(ext[0], HALF, 1)
    mid = pltpu.roll(ext[1], HALF, 1)
    right = pltpu.roll(ext[2], HALF, 1)
    low = jnp.where(lane < HALF, left, mid)
    high = jnp.where(lane < HALF, mid, right)
    for j in range(TAPS):
        moved = jnp.where(lane < j, high, low)
        if j:
            moved = pltpu.roll(moved, 128 - j, 1)
        for rb in range(12):
            block = moved[rb * 16 : rb * 16 + 16]
            if rb < 8:
                spread[rb * 1024 + j * 16 : rb * 1024 + j * 16 + 16, 0:128] = block
            if rb >= 4:
                at = (rb - 4) * 1024 + j * 16
                spread[at : at + 16, 128:256] = block


def kernel(
    raster_ref, trans_ref, kern_ref, weight_ref, lib_ref, tile_ref, corner_ref,
    aerial_ref, score_ref,
    mask, ext, raw_taps, perm, taps, spread, row_basis, col_basis, select,
    lib_raw, units, slots, parts, sums, clips, runs, ring_lse, plane_lse,
    halo_send, halo_recv, lib_sem, pair_send, pair_recv,
    line_send, line_recv, sum_send, sum_recv, all_send, all_recv,
    ring_send, ring_recv, plane_send, plane_recv,
):
    w, n = place()
    g = w // 4
    core = w % 2
    line_me = (w % 4) * 4 + n
    z_me = n * 2 + (w // 2) % 2
    around = [around_peer(w, n, d) for d in AROUND]
    line = [line_peer(w, n, d) for d in LINE]
    plane = [plane_peer(w, n, d) for d in PLANE]
    ring = [line_peer(w, n, (d, 0)) for d in RING]

    barrier = pltpu.get_barrier_semaphore()
    peers = around + line + plane
    for peer in peers:
        pl.semaphore_signal(barrier, inc=1, device_id=peer, device_id_type=MESH)
    lib_copy = pltpu.make_async_copy(lib_ref, lib_raw, lib_sem)
    lib_copy.start()
    mask[...] = (raster_ref[...].astype(F32) * trans_ref[...].astype(F32)).astype(BF16)
    ext[1, HALF : HALF + TILE, :] = mask[...]
    build_taps(kern_ref, raw_taps, perm, taps)
    pl.semaphore_wait(barrier, len(peers))

    def send(src, dst, ssem, rsem, peer):
        copy = pltpu.make_async_remote_copy(
            src_ref=src, dst_ref=dst, send_sem=ssem, recv_sem=rsem,
            device_id=peer, device_id_type=MESH,
        )
        copy.start()
        return copy

    halo = []
    for i, (dw, dn) in enumerate(AROUND):
        src = {0: mask, 1: mask.at[TILE - HALF : TILE], -1: mask.at[0:HALF]}[dn]
        to = {0: slice(HALF, HALF + TILE), 1: slice(0, HALF), -1: slice(HALF + TILE, 2 * HALF + TILE)}[dn]
        dst = ext.at[1 - dw, to]
        halo.append(send(src, dst, halo_send.at[i], halo_recv.at[i], around[i]))

    lib_copy.wait()

    def normal(i, carry):
        at = pl.ds(pl.multiple_of(i * 256, 256), 256)
        units[0, at, :] = unit_rows(lib_raw[at, :].astype(F32))
        return carry

    lax.fori_loop(0, LIB_DEV // 256, normal, 0)
    other = line_peer(w, n, (0, 1))
    pair = send(units.at[0], units.at[1], pair_send, pair_recv, other)
    own_bases(w, n, tile_ref, corner_ref, row_basis, col_basis)
    build_select(w, tile_ref, select)

    for copy in halo:
        copy.wait()
    zero_side = jnp.zeros((192, TILE), BF16)
    zero_rows = jnp.zeros((3, HALF, TILE), BF16)

    @pl.when(w == 0)
    def _():
        ext[0] = zero_side

    @pl.when(w == 63)
    def _():
        ext[2] = zero_side

    @pl.when(n == 0)
    def _():
        ext[:, 0:HALF, :] = zero_rows

    @pl.when(n == 3)
    def _():
        ext[:, HALF + TILE : 2 * HALF + TILE, :] = zero_rows

    shifted_copies(ext, spread)

    field_index = iota((16, 256), 0) // 2
    weight = jnp.zeros((16, 256), F32)
    for k in range(8):
        weight = jnp.where(field_index == k, weight_ref[k], weight)

    def rows(i, carry):
        window = spread[pl.ds(pl.multiple_of(i * 1024, 1024), DEPTH), :]
        both = dot(taps[...], window)
        field = both[0:256] + both[256:512]
        energy = (field * field).reshape(SHIFTS, FIELDS, 256) * weight[None]
        image = jnp.sum(energy, axis=1)
        at = pl.multiple_of(i * 16, 16)
        aerial_ref[pl.ds(at, 16), :] = image[:, 0:128]
        aerial_ref[pl.ds(at + 64, 16), :] = image[:, 128:256]
        return carry

    lax.fori_loop(0, 4, rows, 0)

    halfway = dot(row_basis[...], aerial_ref[...], HIGHEST)
    cross = dot_nt(halfway, col_basis[...], HIGHEST)
    row = iota((256, 256), 0)
    lane = iota((256, 256), 1)
    cross = jnp.where(row // 16 == lane // 16, cross, 0.0)
    fold = (row % 16 == lane % 16).astype(F32)
    wide = jnp.where(row % 16 == lane // 16, dot(cross, fold, HIGHEST), 0.0)
    signature = jnp.sum(wide.reshape(CAP, KSIG, SIGD), axis=1)
    signature = jnp.where(iota((CAP, SIGD), 1) == 0, 0.0, signature)
    slots[line_me] = unit_rows(signature)

    for peer in line:
        send(slots.at[line_me], slots.at[line_me], line_send, line_recv, peer)
    wait_bytes(slots.at[0:15], line_recv)
    picked = dot(select[...], slots[...].reshape(256, SIGD)).astype(BF16)
    parts[...] = picked.reshape(GROUPS, 32, SIGD)

    for i, d in enumerate(PLANE):
        gp = plane[i][0] // 4
        send(parts.at[gp], sums.at[g], sum_send, sum_recv, plane[i])
    sums[g] = parts[g]
    wait_bytes(sums.at[0:15], sum_recv)
    total = sums[0].astype(F32)
    for i in range(1, GROUPS):
        total += sums[i].astype(F32)
    clips[g] = total.astype(BF16)

    for peer in plane:
        send(clips.at[g], clips.at[g], all_send, all_recv, peer)
    pair.wait()
    wait_bytes(clips.at[0:15], all_recv)

    scale = SHARP * math.log2(math.e)
    for half in range(2):
        chosen = clips[half * 8 : half * 8 + 8].reshape(256, SIGD)
        runs[0] = jnp.full((8, 256), -4.0, F32)
        runs[1] = jnp.zeros((8, 256), F32)
        for source in range(2):

            def match(i, carry):
                block = units[source, pl.ds(pl.multiple_of(i * 512, 512), 512), :]
                near = dot_nt(block, chosen).reshape(64, 8, 256)
                old = runs[0]
                top = jnp.maximum(old, jnp.max(near, axis=0))
                gain = jnp.sum(jnp.exp2((near - top[None]) * scale), axis=0)
                runs[1] = runs[1] * jnp.exp2((old - top) * scale) + gain
                runs[0] = top
                return carry

            lax.fori_loop(0, LIB_DEV // 512, match, 0)
        tops = runs[0]
        top = jnp.max(tops, axis=0, keepdims=True)
        weighted = runs[1] * jnp.exp2((tops - top) * scale)
        amount = jnp.sum(weighted, axis=0, keepdims=True)
        ring_lse[z_me, :, half * 256 : half * 256 + 256] = (top - 1.0) * SHARP + jnp.log(amount)

    def joined(parts_ref, count):
        values = [parts_ref[i] for i in range(count)]
        top = values[0]
        for v in values[1:]:
            top = jnp.maximum(top, v)
        amount = jnp.exp(values[0] - top)
        for v in values[1:]:
            amount += jnp.exp(v - top)
        return top + jnp.log(amount)

    for peer in ring:
        send(ring_lse.at[z_me], ring_lse.at[z_me], ring_send, ring_recv, peer)
    wait_bytes(ring_lse.at[0:7], ring_recv)
    plane_lse[g] = joined(ring_lse, 8)
    for peer in plane:
        send(plane_lse.at[g], plane_lse.at[g], plane_send, plane_recv, peer)
    wait_bytes(plane_lse.at[0:15], plane_recv)
    score = joined(plane_lse, GROUPS) / (-SHARP)
    first = g * 32 + ((w // 2) % 2) * 16 + n * 4
    spot = iota((1, OWN_IDS), 1)
    for t in range(4):
        score_ref[t] = jnp.sum(jnp.where(spot == first + t, score, 0.0))

    wait_bytes(slots.at[0:15], line_send)
    wait_bytes(sums.at[0:15], sum_send)
    wait_bytes(clips.at[0:15], all_send)
    wait_bytes(ring_lse.at[0:7], ring_send)
    wait_bytes(plane_lse.at[0:15], plane_send)


def per_device(raster, transmission, kernels, kernel_weight, library, clip_tile, clip_corner):
    vmem = pl.BlockSpec(memory_space=pltpu.VMEM)
    smem = pl.BlockSpec(memory_space=pltpu.SMEM)
    dma = pltpu.SemaphoreType.DMA
    return pl.pallas_call(
        kernel,
        out_shape=(
            jax.ShapeDtypeStruct((TILE, TILE), F32),
            jax.ShapeDtypeStruct((4,), F32),
        ),
        in_specs=[vmem, vmem, vmem, smem, pl.BlockSpec(memory_space=pl.ANY), vmem, vmem],
        out_specs=(vmem, smem),
        scratch_shapes=[
            pltpu.VMEM((TILE, TILE), BF16),
            pltpu.VMEM((3, 192, TILE), BF16),
            pltpu.VMEM((128, 1024), BF16),
            pltpu.VMEM((1024, 1024), BF16),
            pltpu.VMEM((512, DEPTH), BF16),
            pltpu.VMEM((8 * 1024, 256), BF16),
            pltpu.VMEM((256, TILE), F32),
            pltpu.VMEM((256, TILE), F32),
            pltpu.VMEM((OWN_IDS, 256), BF16),
            pltpu.VMEM((LIB_DEV, SIGD), BF16),
            pltpu.VMEM((2, LIB_DEV, SIGD), BF16),
            pltpu.VMEM((16, CAP, SIGD), BF16),
            pltpu.VMEM((GROUPS, 32, SIGD), BF16),
            pltpu.VMEM((GROUPS, 32, SIGD), BF16),
            pltpu.VMEM((GROUPS, 32, SIGD), BF16),
            pltpu.VMEM((2, 8, 256), F32),
            pltpu.VMEM((8, 1, OWN_IDS), F32),
            pltpu.VMEM((GROUPS, 1, OWN_IDS), F32),
            dma((8,)), dma((8,)), dma, dma, dma,
            dma, dma, dma, dma, dma, dma, dma, dma, dma, dma,
        ],
        compiler_params=pltpu.CompilerParams(
            collective_id=0, has_side_effects=True, vmem_limit_bytes=56 * 1024 * 1024
        ),
    )(
        raster,
        transmission,
        kernels.reshape(FIELDS * TAPS, TAPS),
        kernel_weight,
        library,
        clip_tile.reshape(8, 128),
        clip_corner,
    )


def solution(mesh):
    placed = (
        P("narrow", "wide"),
        P("narrow", "wide"),
        P(),
        P(),
        P(("wide", "narrow"), None),
        P(),
        P(),
    )
    return jax.shard_map(
        per_device,
        mesh=mesh,
        in_specs=placed,
        out_specs=(P("narrow", "wide"), P(("wide", "narrow"))),
        check_vma=False,
    )
```

```python
import math

import jax
import jax.numpy as jnp
from jax import lax
from jax.experimental import pallas as pl
from jax.experimental.pallas import tpu as pltpu
from jax.sharding import PartitionSpec as P

TILE = 128
TAPS = 64
HALF = 32
KSIG = 16
CAP = 16
SIGD = 256
FIELDS = 16
SHIFTS = 16
DEPTH = 5 * 1024
GROUPS = 16
OWN_IDS = 512
CLIPS = 1024
LIB_DEV = 2048
SHARP = 400.0
F32 = jnp.float32
BF16 = jnp.bfloat16
I32 = jnp.int32
MESH = pl.DeviceIdType.MESH
HIGHEST = lax.Precision.HIGHEST

PLANE = sorted(
    [(dx, dy) for dx in range(4) for dy in range(4) if dx or dy],
    key=lambda d: -(min(d[0], 4 - d[0]) + min(d[1], 4 - d[1])),
)
LINE = sorted(
    [(dz, dc) for dz in range(8) for dc in range(2) if dz or dc],
    key=lambda d: -(2 * min(d[0], 8 - d[0]) + d[1]),
)
SAME_CORE = sorted(
    [(dx, dy, dz) for dx in range(4) for dy in range(4) for dz in range(8) if dx or dy or dz],
    key=lambda d: -(min(d[0], 4 - d[0]) + min(d[1], 4 - d[1]) + min(d[2], 8 - d[2])),
)
AROUND = [(dw, dn) for dw in (1, -1, 0) for dn in (1, -1, 0) if dw or dn]


def place():
    w = lax.axis_index("wide")
    n = lax.axis_index("narrow")
    return w, n


def plane_peer(w, n, d):
    g = w // 4
    x = (g // 4 + d[0]) % 4
    y = (g % 4 + d[1]) % 4
    return (x * 4 + y) * 4 + w % 4, n


def line_peer(w, n, d):
    z = (n * 2 + (w // 2) % 2 + d[0]) % 8
    c = (w % 2 + d[1]) % 2
    return (w // 4) * 4 + (z % 2) * 2 + c, z // 2


def same_core_peer(w, n, d):
    w, n = plane_peer(w, n, d[:2])
    return line_peer(w, n, (d[2], 0))


def around_peer(w, n, d):
    return (w + d[0] + 64) % 64, (n + d[1] + 4) % 4


def iota(shape, dim):
    return lax.broadcasted_iota(I32, shape, dim)


def dot(a, b, precision=None):
    return jnp.dot(a, b, preferred_element_type=F32, precision=precision)


def dot_nt(a, b, precision=None):
    return lax.dot_general(
        a, b, (((1,), (1,)), ((), ())), preferred_element_type=F32, precision=precision
    )


def wait_bytes(ref, sem):
    pltpu.make_async_copy(ref, ref, sem).wait()


def unit_rows(matrix):
    mean_square = jnp.mean(matrix * matrix, axis=1, keepdims=True)
    return (matrix / (KSIG * jnp.sqrt(mean_square + 1e-06))).astype(BF16)


def build_taps(kern_ref, raw_taps, perm, taps):
    for block in range(8):
        p = iota((128, 1024), 0) + block * 128
        q = iota((128, 1024), 1)
        hit = q == (p % 64) * 16 + p // 64
        perm[block * 128 : block * 128 + 128, :] = jnp.where(hit, 1.0, 0.0).astype(BF16)
    for i in range(0, TAPS, 2):
        pair = jnp.concatenate(
            [kern_ref[pl.ds(i, 16, stride=64), :], kern_ref[pl.ds(i + 1, 16, stride=64), :]],
            axis=1,
        )
        high = pair.astype(BF16)
        low = (pair - high.astype(F32)).astype(BF16)
        row = (i // 16) * 32
        lane = (i % 16) * 64
        raw_taps[row : row + 16, lane : lane + 128] = high
        raw_taps[row + 16 : row + 32, lane : lane + 128] = low
    raw_taps[...] = dot(raw_taps[...], perm[...]).astype(BF16)

    def shift(s, carry):
        inner = iota((32, 128), 1) % 16
        wrap = inner >= 16 - s
        row = pl.multiple_of(s * 16, 16)
        for v in range(8):
            lanes = slice(v * 128, v * 128 + 128)
            for ib in range(5):
                zero = jnp.zeros((32, 128), BF16)
                here = raw_taps[ib * 32 : ib * 32 + 32, lanes] if ib < 4 else zero
                if ib > 0:
                    last = pltpu.roll(raw_taps[ib * 32 - 32 : ib * 32, lanes], 112, 1)
                else:
                    last = zero
                moved = pltpu.roll(jnp.where(wrap, last, here), s, 1)
                to = slice(ib * 1024 + v * 128, ib * 1024 + v * 128 + 128)
                taps[pl.ds(row, 16), to] = moved[0:16]
                taps[pl.ds(row + 256, 16), to] = moved[16:32]
        return carry

    lax.fori_loop(0, SHIFTS, shift, 0)


def cosine(m):
    v = (64 - jnp.abs(m - 128)).astype(F32) * (math.pi / 128)
    s = v * v
    poly = 1.0 / 6227020800.0
    for c in (-1.0 / 39916800, 1.0 / 362880, -1.0 / 5040, 1.0 / 120, -1.0 / 6, 1.0):
        poly = poly * s + c
    return -(v * poly)


def shifted_basis(corner):
    spread = (iota((256, 16), 0) // 16 == iota((256, 16), 1)).astype(F32)
    corners = dot(spread, jnp.broadcast_to(corner, (16, 128))).astype(I32)
    k = iota((256, 128), 0) % 16
    offset = iota((256, 128), 1) - corners
    inside = (offset >= 0) & (offset < 64)
    weight = jnp.where(k == 0, math.sqrt(1.0 / 64), math.sqrt(2.0 / 64)).astype(F32)
    m = jnp.where(inside, ((2 * offset + 1) * k) % 256, 0)
    return jnp.where(inside, weight * cosine(m), 0.0)


def own_bases(w, n, tile_ref, corner_ref, row_basis, col_basis):
    owned = (tile_ref[...] == n * 64 + w).astype(F32)
    earlier = (iota((128, 128), 0) < iota((128, 128), 1)).astype(F32)
    before = dot(owned, earlier)
    base = jnp.zeros((1, 1), F32)
    slot = iota((16, 128), 0).astype(F32)
    rows = jnp.zeros((16, 128), F32)
    cols = jnp.zeros((16, 128), F32)
    for r in range(8):
        own = owned[r : r + 1]
        here = (own > 0) & (before[r : r + 1] + base == slot)
        part = slice(r * 128, r * 128 + 128)
        rows += jnp.where(here, corner_ref[0:1, part].astype(F32), 0.0)
        cols += jnp.where(here, corner_ref[1:2, part].astype(F32), 0.0)
        base += jnp.sum(own, axis=1, keepdims=True)
    row_basis[...] = shifted_basis(jnp.sum(rows, axis=1, keepdims=True))
    col_basis[...] = shifted_basis(jnp.sum(cols, axis=1, keepdims=True))


def build_select(w, tile_ref, select):
    core = w % 2
    q = iota((64, 256), 1)
    dev = q // 16
    slot_key = ((dev % 4) * 64 + (w // 4) * 4 + dev // 4) * 16 + q % 16
    for r in range(8):
        m = iota((64, 128), 0) + r * 64
        ids = (m // 16) * 32 + core * 16 + m % 16
        lane = iota((64, 128), 1)
        tiles = tile_ref[r : r + 1, :]
        mine = jnp.sum(
            jnp.where(ids == lane + r * 128, tiles.astype(F32), 0.0), axis=1, keepdims=True
        )
        rank = jnp.zeros((64, 128), F32)
        for b in range(r + 1):
            same = tile_ref[b : b + 1, :].astype(F32) == mine
            if b == r:
                same = same & (lane + r * 128 < ids)
            rank += jnp.where(same, 1.0, 0.0)
        key = (mine * 16.0 + jnp.sum(rank, axis=1, keepdims=True)).astype(I32)
        select[r * 64 : r * 64 + 64, :] = (key == slot_key).astype(F32).astype(BF16)


def shifted_copies(ext, spread):
    lane = iota((192, 128), 1)
    left = pltpu.roll(ext[0], HALF, 1)
    mid = pltpu.roll(ext[1], HALF, 1)
    right = pltpu.roll(ext[2], HALF, 1)
    low = jnp.where(lane < HALF, left, mid)
    high = jnp.where(lane < HALF, mid, right)
    for j in range(TAPS):
        moved = jnp.where(lane < j, high, low)
        if j:
            moved = pltpu.roll(moved, 128 - j, 1)
        for rb in range(12):
            block = moved[rb * 16 : rb * 16 + 16]
            if rb < 8:
                spread[rb * 1024 + j * 16 : rb * 1024 + j * 16 + 16, 0:128] = block
            if rb >= 4:
                at = (rb - 4) * 1024 + j * 16
                spread[at : at + 16, 128:256] = block


def kernel(
    raster_ref, trans_ref, kern_ref, weight_ref, lib_ref, tile_ref, corner_ref,
    aerial_ref, score_ref,
    mask, ext, raw_taps, perm, taps, spread, row_basis, col_basis, select,
    lib_raw, units, slots, parts, sums, clips, turned, own_lse, all_lse,
    halo_send, halo_recv, lib_sem, pair_send, pair_recv,
    line_send, line_recv, sum_send, sum_recv, all_send, all_recv,
    lse_send, lse_recv,
):
    w, n = place()
    g = w // 4
    core = w % 2
    line_me = (w % 4) * 4 + n
    me = g * 8 + n * 2 + (w // 2) % 2
    around = [around_peer(w, n, d) for d in AROUND]
    line = [line_peer(w, n, d) for d in LINE]
    plane = [plane_peer(w, n, d) for d in PLANE]

    barrier = pltpu.get_barrier_semaphore()
    peers = around + line + plane
    for peer in peers:
        pl.semaphore_signal(barrier, inc=1, device_id=peer, device_id_type=MESH)
    lib_copy = pltpu.make_async_copy(lib_ref, lib_raw, lib_sem)
    lib_copy.start()
    mask[...] = (raster_ref[...].astype(F32) * trans_ref[...].astype(F32)).astype(BF16)
    ext[1, HALF : HALF + TILE, :] = mask[...]
    build_taps(kern_ref, raw_taps, perm, taps)
    pl.semaphore_wait(barrier, len(peers))

    def send(src, dst, ssem, rsem, peer):
        copy = pltpu.make_async_remote_copy(
            src_ref=src, dst_ref=dst, send_sem=ssem, recv_sem=rsem,
            device_id=peer, device_id_type=MESH,
        )
        copy.start()
        return copy

    halo = []
    for i, (dw, dn) in enumerate(AROUND):
        src = {0: mask, 1: mask.at[TILE - HALF : TILE], -1: mask.at[0:HALF]}[dn]
        to = {0: slice(HALF, HALF + TILE), 1: slice(0, HALF), -1: slice(HALF + TILE, 2 * HALF + TILE)}[dn]
        dst = ext.at[1 - dw, to]
        halo.append(send(src, dst, halo_send.at[i], halo_recv.at[i], around[i]))

    lib_copy.wait()

    def normal(i, carry):
        at = pl.ds(pl.multiple_of(i * 256, 256), 256)
        units[0, at, :] = unit_rows(lib_raw[at, :].astype(F32))
        return carry

    lax.fori_loop(0, LIB_DEV // 256, normal, 0)
    other = line_peer(w, n, (0, 1))
    pair = send(units.at[0], units.at[1], pair_send, pair_recv, other)
    own_bases(w, n, tile_ref, corner_ref, row_basis, col_basis)
    build_select(w, tile_ref, select)

    for copy in halo:
        copy.wait()
    zero_side = jnp.zeros((192, TILE), BF16)
    zero_rows = jnp.zeros((3, HALF, TILE), BF16)

    @pl.when(w == 0)
    def _():
        ext[0] = zero_side

    @pl.when(w == 63)
    def _():
        ext[2] = zero_side

    @pl.when(n == 0)
    def _():
        ext[:, 0:HALF, :] = zero_rows

    @pl.when(n == 3)
    def _():
        ext[:, HALF + TILE : 2 * HALF + TILE, :] = zero_rows

    shifted_copies(ext, spread)

    field_index = iota((16, 256), 0) // 2
    weight = jnp.zeros((16, 256), F32)
    for k in range(8):
        weight = jnp.where(field_index == k, weight_ref[k], weight)

    def rows(i, carry):
        window = spread[pl.ds(pl.multiple_of(i * 1024, 1024), DEPTH), :]
        both = dot(taps[...], window)
        field = both[0:256] + both[256:512]
        energy = (field * field).reshape(SHIFTS, FIELDS, 256) * weight[None]
        image = jnp.sum(energy, axis=1)
        at = pl.multiple_of(i * 16, 16)
        aerial_ref[pl.ds(at, 16), :] = image[:, 0:128]
        aerial_ref[pl.ds(at + 64, 16), :] = image[:, 128:256]
        return carry

    lax.fori_loop(0, 4, rows, 0)

    halfway = dot(row_basis[...], aerial_ref[...], HIGHEST)
    cross = dot_nt(halfway, col_basis[...], HIGHEST)
    row = iota((256, 256), 0)
    lane = iota((256, 256), 1)
    cross = jnp.where(row // 16 == lane // 16, cross, 0.0)
    fold = (row % 16 == lane % 16).astype(F32)
    wide = jnp.where(row % 16 == lane // 16, dot(cross, fold, HIGHEST), 0.0)
    signature = jnp.sum(wide.reshape(CAP, KSIG, SIGD), axis=1)
    signature = jnp.where(iota((CAP, SIGD), 1) == 0, 0.0, signature)
    slots[line_me] = unit_rows(signature)

    for peer in line:
        send(slots.at[line_me], slots.at[line_me], line_send, line_recv, peer)
    wait_bytes(slots.at[0:15], line_recv)
    picked = dot(select[...], slots[...].reshape(256, SIGD)).astype(BF16)
    parts[...] = picked.reshape(GROUPS, 32, SIGD)

    for i, d in enumerate(PLANE):
        gp = plane[i][0] // 4
        send(parts.at[gp], sums.at[g], sum_send, sum_recv, plane[i])
    sums[g] = parts[g]
    wait_bytes(sums.at[0:15], sum_recv)
    total = sums[0].astype(F32)
    for i in range(1, GROUPS):
        total += sums[i].astype(F32)
    clips[g] = total.astype(BF16)

    for peer in plane:
        send(clips.at[g], clips.at[g], all_send, all_recv, peer)
    pair.wait()
    wait_bytes(clips.at[0:15], all_recv)

    scale = SHARP * math.log2(math.e)
    turned[...] = jnp.transpose(clips[...].reshape(OWN_IDS, SIGD))
    tops = jnp.full((8, OWN_IDS), -4.0, F32)
    sums_of = jnp.zeros((8, OWN_IDS), F32)
    for block in range(2 * LIB_DEV // 512):
        at = (block % 4) * 512
        near = dot(units[block // 4, at : at + 512, :], turned[...]).reshape(64, 8, OWN_IDS)
        old = tops
        tops = jnp.maximum(old, jnp.max(near, axis=0))
        gain = jnp.sum(jnp.exp2((near - tops[None]) * scale), axis=0)
        sums_of = sums_of * jnp.exp2((old - tops) * scale) + gain
    top = jnp.max(tops, axis=0, keepdims=True)
    amount = jnp.sum(sums_of * jnp.exp2((tops - top) * scale), axis=0, keepdims=True)
    found = (top - 1.0) * SHARP + jnp.log(amount)
    for block in range(4):
        own_lse[block] = found[:, block * 128 : block * 128 + 128]

    for d in SAME_CORE:
        peer = same_core_peer(w, n, d)
        send(own_lse.at[peer[0] // 16], all_lse.at[me], lse_send, lse_recv, peer)
    all_lse[me] = own_lse[g // 4]
    wait_bytes(all_lse.at[0:127], lse_recv)
    every = all_lse[...]
    top = jnp.max(every, axis=0)
    score = (top + jnp.log(jnp.sum(jnp.exp(every - top[None]), axis=0))) / (-SHARP)
    first = (g % 4) * 32 + ((w // 2) % 2) * 16 + n * 4
    spot = iota((1, 128), 1)
    for t in range(4):
        score_ref[t] = jnp.sum(jnp.where(spot == first + t, score, 0.0))

    wait_bytes(slots.at[0:15], line_send)
    wait_bytes(sums.at[0:15], sum_send)
    wait_bytes(clips.at[0:15], all_send)
    wait_bytes(all_lse.at[0:127], lse_send)


def per_device(raster, transmission, kernels, kernel_weight, library, clip_tile, clip_corner):
    vmem = pl.BlockSpec(memory_space=pltpu.VMEM)
    smem = pl.BlockSpec(memory_space=pltpu.SMEM)
    dma = pltpu.SemaphoreType.DMA
    return pl.pallas_call(
        kernel,
        out_shape=(
            jax.ShapeDtypeStruct((TILE, TILE), F32),
            jax.ShapeDtypeStruct((4,), F32),
        ),
        in_specs=[vmem, vmem, vmem, smem, pl.BlockSpec(memory_space=pl.ANY), vmem, vmem],
        out_specs=(vmem, smem),
        scratch_shapes=[
            pltpu.VMEM((TILE, TILE), BF16),
            pltpu.VMEM((3, 192, TILE), BF16),
            pltpu.VMEM((128, 1024), BF16),
            pltpu.VMEM((1024, 1024), BF16),
            pltpu.VMEM((512, DEPTH), BF16),
            pltpu.VMEM((8 * 1024, 256), BF16),
            pltpu.VMEM((256, TILE), F32),
            pltpu.VMEM((256, TILE), F32),
            pltpu.VMEM((OWN_IDS, 256), BF16),
            pltpu.VMEM((LIB_DEV, SIGD), BF16),
            pltpu.VMEM((2, LIB_DEV, SIGD), BF16),
            pltpu.VMEM((16, CAP, SIGD), BF16),
            pltpu.VMEM((GROUPS, 32, SIGD), BF16),
            pltpu.VMEM((GROUPS, 32, SIGD), BF16),
            pltpu.VMEM((GROUPS, 32, SIGD), BF16),
            pltpu.VMEM((SIGD, OWN_IDS), BF16),
            pltpu.VMEM((4, 1, 128), F32),
            pltpu.VMEM((128, 1, 128), F32),
            dma((8,)), dma((8,)), dma, dma, dma,
            dma, dma, dma, dma, dma, dma, dma, dma,
        ],
        compiler_params=pltpu.CompilerParams(
            collective_id=0, has_side_effects=True, vmem_limit_bytes=56 * 1024 * 1024
        ),
    )(
        raster,
        transmission,
        kernels.reshape(FIELDS * TAPS, TAPS),
        kernel_weight,
        library,
        clip_tile.reshape(8, 128),
        clip_corner,
    )


def solution(mesh):
    placed = (
        P("narrow", "wide"),
        P("narrow", "wide"),
        P(),
        P(),
        P(("wide", "narrow"), None),
        P(),
        P(),
    )
    return jax.shard_map(
        per_device,
        mesh=mesh,
        in_specs=placed,
        out_specs=(P("narrow", "wide"), P(("wide", "narrow"))),
        check_vma=False,
    )
```

```python
import math

import jax
import jax.numpy as jnp
from jax import lax
from jax.experimental import pallas as pl
from jax.experimental.pallas import tpu as pltpu
from jax.sharding import PartitionSpec as P

TILE = 128
TAPS = 64
HALF = 32
KSIG = 16
CAP = 16
SIGD = 256
FIELDS = 16
SHIFTS = 16
DEPTH = 5 * 1024
GROUPS = 16
OWN_IDS = 512
CLIPS = 1024
LIB_DEV = 2048
SHARP = 400.0
F32 = jnp.float32
BF16 = jnp.bfloat16
I32 = jnp.int32
MESH = pl.DeviceIdType.MESH
HIGHEST = lax.Precision.HIGHEST

PLANE = sorted(
    [(dx, dy) for dx in range(4) for dy in range(4) if dx or dy],
    key=lambda d: -(min(d[0], 4 - d[0]) + min(d[1], 4 - d[1])),
)
LINE = sorted(
    [(dz, dc) for dz in range(8) for dc in range(2) if dz or dc],
    key=lambda d: -(2 * min(d[0], 8 - d[0]) + d[1]),
)
SAME_CORE = sorted(
    [(dx, dy, dz) for dx in range(4) for dy in range(4) for dz in range(8) if dx or dy or dz],
    key=lambda d: -(min(d[0], 4 - d[0]) + min(d[1], 4 - d[1]) + min(d[2], 8 - d[2])),
)
AROUND = [(1, 0), (-1, 0), (0, 1), (0, -1)]


def place():
    w = lax.axis_index("wide")
    n = lax.axis_index("narrow")
    return w, n


def plane_peer(w, n, d):
    g = w // 4
    x = (g // 4 + d[0]) % 4
    y = (g % 4 + d[1]) % 4
    return (x * 4 + y) * 4 + w % 4, n


def line_peer(w, n, d):
    z = (n * 2 + (w // 2) % 2 + d[0]) % 8
    c = (w % 2 + d[1]) % 2
    return (w // 4) * 4 + (z % 2) * 2 + c, z // 2


def same_core_peer(w, n, d):
    w, n = plane_peer(w, n, d[:2])
    return line_peer(w, n, (d[2], 0))


def around_peer(w, n, d):
    return (w + d[0] + 64) % 64, (n + d[1] + 4) % 4


def iota(shape, dim):
    return lax.broadcasted_iota(I32, shape, dim)


def dot(a, b, precision=None):
    return jnp.dot(a, b, preferred_element_type=F32, precision=precision)


def dot_nt(a, b, precision=None):
    return lax.dot_general(
        a, b, (((1,), (1,)), ((), ())), preferred_element_type=F32, precision=precision
    )


def wait_bytes(ref, sem):
    pltpu.make_async_copy(ref, ref, sem).wait()


def unit_rows(matrix):
    mean_square = jnp.mean(matrix * matrix, axis=1, keepdims=True)
    return (matrix / (KSIG * jnp.sqrt(mean_square + 1e-06))).astype(BF16)


def build_taps(kern_ref, raw_taps, perm, taps):
    for block in range(8):
        p = iota((128, 1024), 0) + block * 128
        q = iota((128, 1024), 1)
        hit = q == (p % 64) * 16 + p // 64
        perm[block * 128 : block * 128 + 128, :] = jnp.where(hit, 1.0, 0.0).astype(BF16)
    for i in range(0, TAPS, 2):
        pair = jnp.concatenate(
            [kern_ref[pl.ds(i, 16, stride=64), :], kern_ref[pl.ds(i + 1, 16, stride=64), :]],
            axis=1,
        )
        high = pair.astype(BF16)
        low = (pair - high.astype(F32)).astype(BF16)
        row = (i // 16) * 32
        lane = (i % 16) * 64
        raw_taps[row : row + 16, lane : lane + 128] = high
        raw_taps[row + 16 : row + 32, lane : lane + 128] = low
    raw_taps[...] = dot(raw_taps[...], perm[...]).astype(BF16)

    def shift(s, carry):
        inner = iota((32, 128), 1) % 16
        wrap = inner >= 16 - s
        row = pl.multiple_of(s * 16, 16)
        for v in range(8):
            lanes = slice(v * 128, v * 128 + 128)
            for ib in range(5):
                zero = jnp.zeros((32, 128), BF16)
                here = raw_taps[ib * 32 : ib * 32 + 32, lanes] if ib < 4 else zero
                if ib > 0:
                    last = pltpu.roll(raw_taps[ib * 32 - 32 : ib * 32, lanes], 112, 1)
                else:
                    last = zero
                moved = pltpu.roll(jnp.where(wrap, last, here), s, 1)
                to = slice(ib * 1024 + v * 128, ib * 1024 + v * 128 + 128)
                taps[pl.ds(row, 16), to] = moved[0:16]
                taps[pl.ds(row + 256, 16), to] = moved[16:32]
        return carry

    lax.fori_loop(0, SHIFTS, shift, 0)


def cosine(m):
    v = (64 - jnp.abs(m - 128)).astype(F32) * (math.pi / 128)
    s = v * v
    poly = 1.0 / 6227020800.0
    for c in (-1.0 / 39916800, 1.0 / 362880, -1.0 / 5040, 1.0 / 120, -1.0 / 6, 1.0):
        poly = poly * s + c
    return -(v * poly)


def shifted_basis(corner):
    spread = (iota((256, 16), 0) // 16 == iota((256, 16), 1)).astype(F32)
    corners = dot(spread, jnp.broadcast_to(corner, (16, 128))).astype(I32)
    k = iota((256, 128), 0) % 16
    offset = iota((256, 128), 1) - corners
    inside = (offset >= 0) & (offset < 64)
    weight = jnp.where(k == 0, math.sqrt(1.0 / 64), math.sqrt(2.0 / 64)).astype(F32)
    m = jnp.where(inside, ((2 * offset + 1) * k) % 256, 0)
    return jnp.where(inside, weight * cosine(m), 0.0)


def own_bases(w, n, tile_ref, corner_ref, row_basis, col_basis):
    owned = (tile_ref[...] == n * 64 + w).astype(F32)
    earlier = (iota((128, 128), 0) < iota((128, 128), 1)).astype(F32)
    before = dot(owned, earlier)
    base = jnp.zeros((1, 1), F32)
    slot = iota((16, 128), 0).astype(F32)
    rows = jnp.zeros((16, 128), F32)
    cols = jnp.zeros((16, 128), F32)
    for r in range(8):
        own = owned[r : r + 1]
        here = (own > 0) & (before[r : r + 1] + base == slot)
        part = slice(r * 128, r * 128 + 128)
        rows += jnp.where(here, corner_ref[0:1, part].astype(F32), 0.0)
        cols += jnp.where(here, corner_ref[1:2, part].astype(F32), 0.0)
        base += jnp.sum(own, axis=1, keepdims=True)
    row_basis[...] = shifted_basis(jnp.sum(rows, axis=1, keepdims=True))
    col_basis[...] = shifted_basis(jnp.sum(cols, axis=1, keepdims=True))


def build_select(w, tile_ref, select):
    core = w % 2
    q = iota((64, 256), 1)
    dev = q // 16
    slot_key = ((dev % 4) * 64 + (w // 4) * 4 + dev // 4) * 16 + q % 16
    for r in range(8):
        m = iota((64, 128), 0) + r * 64
        ids = (m // 16) * 32 + core * 16 + m % 16
        lane = iota((64, 128), 1)
        tiles = tile_ref[r : r + 1, :]
        mine = jnp.sum(
            jnp.where(ids == lane + r * 128, tiles.astype(F32), 0.0), axis=1, keepdims=True
        )
        rank = jnp.zeros((64, 128), F32)
        for b in range(r + 1):
            same = tile_ref[b : b + 1, :].astype(F32) == mine
            if b == r:
                same = same & (lane + r * 128 < ids)
            rank += jnp.where(same, 1.0, 0.0)
        key = (mine * 16.0 + jnp.sum(rank, axis=1, keepdims=True)).astype(I32)
        select[r * 64 : r * 64 + 64, :] = (key == slot_key).astype(F32).astype(BF16)


def shifted_copies(left, mid, right, places):
    lane = iota(mid.shape, 1)
    mid = pltpu.roll(mid, HALF, 1)
    low = jnp.where(lane < HALF, left, mid)
    high = jnp.where(lane < HALF, mid, right)
    for j in range(TAPS):
        moved = jnp.where(lane < j, high, low)
        if j:
            moved = pltpu.roll(moved, 128 - j, 1)
        for b, where in enumerate(places):
            for ref, index, at in where:
                row = index * 1024 + j * 16
                ref[row : row + 16, at : at + 128] = moved[b * 16 : b * 16 + 16]


def rolled(x, shift):
    return pltpu.roll(x, shift % 128, 1) if shift % 128 else x


def pack_side(mask, first):
    lane = iota((HALF, TILE), 1)
    packed = jnp.zeros((HALF, TILE), BF16)
    for q in range(4):
        moved = rolled(mask[q * 32 : q * 32 + 32, :], q * 32 - first)
        packed = jnp.where(lane // 32 == q, moved, packed)
    return packed


def kernel(
    raster_hbm, trans_hbm, kern_hbm, weight_hbm, lib_ref, tile_hbm, corner_hbm,
    aerial_ref, score_ref,
    raster_ref, trans_ref, kern_ref, weight_ref, tile_ref, corner_ref, in_sem,
    mask, packed, side, edge, corner, raw_taps, perm, taps, inner, outer, row_basis, col_basis, select,
    lib_raw, units, slots, parts, sums, clips, turned, own_lse, all_lse,
    halo_send, halo_recv, corner_send, corner_recv, lib_sem, pair_send, pair_recv,
    line_send, line_recv, sum_send, sum_recv, all_send, all_recv,
    lse_send, lse_recv,
):
    w, n = place()
    g = w // 4
    core = w % 2
    line_me = (w % 4) * 4 + n
    me = g * 8 + n * 2 + (w // 2) % 2
    around = [around_peer(w, n, d) for d in AROUND]
    line = [line_peer(w, n, d) for d in LINE]
    plane = [plane_peer(w, n, d) for d in PLANE]

    barrier = pltpu.get_barrier_semaphore()
    peers = around + line + plane
    for peer in peers:
        pl.semaphore_signal(barrier, inc=1, device_id=peer, device_id_type=MESH)
    inputs = [
        pltpu.make_async_copy(src, dst, in_sem.at[i])
        for i, (src, dst) in enumerate([
            (raster_hbm, raster_ref), (trans_hbm, trans_ref), (kern_hbm, kern_ref),
            (weight_hbm, weight_ref), (tile_hbm, tile_ref), (corner_hbm, corner_ref),
        ])
    ]
    for copy in inputs:
        copy.start()
    lib_copy = pltpu.make_async_copy(lib_ref, lib_raw, lib_sem)
    lib_copy.start()
    for copy in inputs:
        copy.wait()
    mask[...] = (raster_ref[...].astype(F32) * trans_ref[...].astype(F32)).astype(BF16)
    packed[0] = pack_side(mask[...], 0)
    packed[1] = pack_side(mask[...], 96)
    build_taps(kern_ref, raw_taps, perm, taps)
    pl.semaphore_wait(barrier, len(peers))

    def send(src, dst, ssem, rsem, peer):
        copy = pltpu.make_async_remote_copy(
            src_ref=src, dst_ref=dst, send_sem=ssem, recv_sem=rsem,
            device_id=peer, device_id_type=MESH,
        )
        copy.start()
        return copy

    halo = []
    pieces = [(packed.at[1], side.at[0]), (packed.at[0], side.at[1]), (mask.at[96:128], edge.at[0]), (mask.at[0:32], edge.at[1])]
    for i, (src, dst) in enumerate(pieces):
        halo.append(send(src, dst, halo_send.at[i], halo_recv.at[i], around[i]))

    lib_copy.wait()

    def normal(i, carry):
        at = pl.ds(pl.multiple_of(i * 256, 256), 256)
        units[0, at, :] = unit_rows(lib_raw[at, :].astype(F32))
        return carry

    lax.fori_loop(0, LIB_DEV // 256, normal, 0)
    other = line_peer(w, n, (0, 1))
    pair = send(units.at[0], units.at[1], pair_send, pair_recv, other)
    own_bases(w, n, tile_ref, corner_ref, row_basis, col_basis)
    build_select(w, tile_ref, select)

    for copy in halo[:2]:
        copy.wait()

    @pl.when(w == 0)
    def _():
        side[0] = jnp.zeros((HALF, TILE), BF16)

    @pl.when(w == 63)
    def _():
        side[1] = jnp.zeros((HALF, TILE), BF16)

    below, above = around[2], around[3]
    pieces = [(side, corner.at[0], below), (side, corner.at[1], above)]
    corners = []
    for i, (src, dst, peer) in enumerate(pieces):
        corners.append(send(src, dst, corner_send.at[i], corner_recv.at[i], peer))

    places = [[] for _ in range(8)]
    for b in range(8):
        rb = b + 2
        if rb < 8:
            places[b].append((inner, rb - 2, 0))
        if rb >= 4:
            places[b].append((inner, rb - 4, 128))
        places[b].append((outer, rb, 0) if rb < 6 else (outer, rb - 6, 128))
    lefts = jnp.concatenate([rolled(side[0], -32 * q) for q in range(4)], axis=0)
    rights = jnp.concatenate([rolled(side[1], 32 - 32 * q) for q in range(4)], axis=0)
    shifted_copies(lefts, mask[...], rights, places)

    field_index = iota((16, 256), 0) // 2
    weight = jnp.zeros((16, 256), F32)
    for k in range(8):
        weight = jnp.where(field_index == k, weight_ref[k], weight)

    def rows(source, first, second):
        def pair_of_blocks(i, carry):
            window = source[pl.ds(pl.multiple_of(i * 1024, 1024), DEPTH), :]
            both = dot(taps[...], window)
            field = both[0:256] + both[256:512]
            energy = (field * field).reshape(SHIFTS, FIELDS, 256) * weight[None]
            image = jnp.sum(energy, axis=1)
            at = pl.multiple_of(i * 16, 16)
            aerial_ref[pl.ds(at + first * 16, 16), :] = image[:, 0:128]
            aerial_ref[pl.ds(at + second * 16, 16), :] = image[:, 128:256]
            return carry

        lax.fori_loop(0, 2, pair_of_blocks, 0)

    rows(inner, 2, 4)
    for copy in halo[2:] + corners:
        copy.wait()

    @pl.when(n == 0)
    def _():
        edge[0] = jnp.zeros((HALF, TILE), BF16)
        corner[0] = jnp.zeros((2, HALF, TILE), BF16)

    @pl.when(n == 3)
    def _():
        edge[1] = jnp.zeros((HALF, TILE), BF16)
        corner[1] = jnp.zeros((2, HALF, TILE), BF16)

    places = [[(outer, 0, 0)], [(outer, 1, 0)], [(outer, 4, 128)], [(outer, 5, 128)]]
    shifted_copies(
        jnp.concatenate([rolled(corner[0, 0], -96), corner[1, 0]], axis=0),
        edge[...].reshape(2 * HALF, TILE),
        jnp.concatenate([rolled(corner[0, 1], -64), rolled(corner[1, 1], 32)], axis=0),
        places,
    )
    rows(outer, 0, 6)

    halfway = dot(row_basis[...], aerial_ref[...], HIGHEST)
    cross = dot_nt(halfway, col_basis[...], HIGHEST)
    row = iota((256, 256), 0)
    lane = iota((256, 256), 1)
    cross = jnp.where(row // 16 == lane // 16, cross, 0.0)
    fold = (row % 16 == lane % 16).astype(F32)
    wide = jnp.where(row % 16 == lane // 16, dot(cross, fold, HIGHEST), 0.0)
    signature = jnp.sum(wide.reshape(CAP, KSIG, SIGD), axis=1)
    signature = jnp.where(iota((CAP, SIGD), 1) == 0, 0.0, signature)
    slots[line_me] = unit_rows(signature)

    for peer in line:
        send(slots.at[line_me], slots.at[line_me], line_send, line_recv, peer)
    wait_bytes(slots.at[0:15], line_recv)
    picked = dot(select[...], slots[...].reshape(256, SIGD)).astype(BF16)
    parts[...] = picked.reshape(GROUPS, 32, SIGD)

    for i, d in enumerate(PLANE):
        gp = plane[i][0] // 4
        send(parts.at[gp], sums.at[g], sum_send, sum_recv, plane[i])
    sums[g] = parts[g]
    wait_bytes(sums.at[0:15], sum_recv)
    total = sums[0].astype(F32)
    for i in range(1, GROUPS):
        total += sums[i].astype(F32)
    clips[g] = total.astype(BF16)

    for peer in plane:
        send(clips.at[g], clips.at[g], all_send, all_recv, peer)
    pair.wait()
    wait_bytes(clips.at[0:15], all_recv)

    scale = SHARP * math.log2(math.e)
    turned[...] = jnp.transpose(clips[...].reshape(OWN_IDS, SIGD))
    tops = jnp.full((8, OWN_IDS), -4.0, F32)
    sums_of = jnp.zeros((8, OWN_IDS), F32)
    for block in range(2 * LIB_DEV // 512):
        at = (block % 4) * 512
        near = dot(units[block // 4, at : at + 512, :], turned[...]).reshape(64, 8, OWN_IDS)
        old = tops
        tops = jnp.maximum(old, jnp.max(near, axis=0))
        gain = jnp.sum(jnp.exp2((near - tops[None]) * scale), axis=0)
        sums_of = sums_of * jnp.exp2((old - tops) * scale) + gain
    top = jnp.max(tops, axis=0, keepdims=True)
    amount = jnp.sum(sums_of * jnp.exp2((tops - top) * scale), axis=0, keepdims=True)
    found = (top - 1.0) * SHARP + jnp.log(amount)
    for block in range(4):
        own_lse[block] = found[:, block * 128 : block * 128 + 128]

    for d in SAME_CORE:
        peer = same_core_peer(w, n, d)
        send(own_lse.at[peer[0] // 16], all_lse.at[me], lse_send, lse_recv, peer)
    all_lse[me] = own_lse[g // 4]
    wait_bytes(all_lse.at[0:127], lse_recv)
    every = all_lse[...]
    top = jnp.max(every, axis=0)
    score = (top + jnp.log(jnp.sum(jnp.exp(every - top[None]), axis=0))) / (-SHARP)
    first = (g % 4) * 32 + ((w // 2) % 2) * 16 + n * 4
    spot = iota((1, 128), 1)
    for t in range(4):
        score_ref[t] = jnp.sum(jnp.where(spot == first + t, score, 0.0))

    wait_bytes(slots.at[0:15], line_send)
    wait_bytes(sums.at[0:15], sum_send)
    wait_bytes(clips.at[0:15], all_send)
    wait_bytes(all_lse.at[0:127], lse_send)


def per_device(raster, transmission, kernels, kernel_weight, library, clip_tile, clip_corner):
    hbm = pl.BlockSpec(memory_space=pl.ANY)
    smem = pl.BlockSpec(memory_space=pltpu.SMEM)
    dma = pltpu.SemaphoreType.DMA
    return pl.pallas_call(
        kernel,
        out_shape=(pltpu.VMEM((TILE, TILE), F32), jax.ShapeDtypeStruct((4,), F32)),
        in_specs=[hbm] * 7,
        out_specs=(pl.BlockSpec(memory_space=pltpu.VMEM), smem),
        scratch_shapes=[
            pltpu.VMEM((TILE, TILE), I32),
            pltpu.VMEM((TILE, TILE), BF16),
            pltpu.VMEM((FIELDS * TAPS, TAPS), F32),
            pltpu.SMEM((8,), F32),
            pltpu.VMEM((8, 128), I32),
            pltpu.VMEM((2, CLIPS), I32),
            dma((6,)),
            pltpu.VMEM((TILE, TILE), BF16),
            pltpu.VMEM((2, HALF, TILE), BF16),
            pltpu.VMEM((2, HALF, TILE), BF16),
            pltpu.VMEM((2, HALF, TILE), BF16),
            pltpu.VMEM((2, 2, HALF, TILE), BF16),
            pltpu.VMEM((128, 1024), BF16),
            pltpu.VMEM((1024, 1024), BF16),
            pltpu.VMEM((512, DEPTH), BF16),
            pltpu.VMEM((6 * 1024, 256), BF16),
            pltpu.VMEM((6 * 1024, 256), BF16),
            pltpu.VMEM((256, TILE), F32),
            pltpu.VMEM((256, TILE), F32),
            pltpu.VMEM((OWN_IDS, 256), BF16),
            pltpu.VMEM((LIB_DEV, SIGD), BF16),
            pltpu.VMEM((2, LIB_DEV, SIGD), BF16),
            pltpu.VMEM((16, CAP, SIGD), BF16),
            pltpu.VMEM((GROUPS, 32, SIGD), BF16),
            pltpu.VMEM((GROUPS, 32, SIGD), BF16),
            pltpu.VMEM((GROUPS, 32, SIGD), BF16),
            pltpu.VMEM((SIGD, OWN_IDS), BF16),
            pltpu.VMEM((4, 1, 128), F32),
            pltpu.VMEM((128, 1, 128), F32),
            dma((4,)), dma((4,)), dma((2,)), dma((2,)), dma, dma, dma,
            dma, dma, dma, dma, dma, dma, dma, dma,
        ],
        compiler_params=pltpu.CompilerParams(
            collective_id=0, has_side_effects=True, vmem_limit_bytes=56 * 1024 * 1024
        ),
    )(
        raster,
        transmission,
        kernels.reshape(FIELDS * TAPS, TAPS),
        kernel_weight,
        library,
        clip_tile.reshape(8, 128),
        clip_corner,
    )


def solution(mesh):
    placed = (
        P("narrow", "wide"),
        P("narrow", "wide"),
        P(),
        P(),
        P(("wide", "narrow"), None),
        P(),
        P(),
    )
    return jax.shard_map(
        per_device,
        mesh=mesh,
        in_specs=placed,
        out_specs=(P("narrow", "wide"), P(("wide", "narrow"))),
        check_vma=False,
    )
```

```python
import math

import jax
import jax.numpy as jnp
from jax import lax
from jax.experimental import pallas as pl
from jax.experimental.pallas import tpu as pltpu
from jax.sharding import PartitionSpec as P

TILE = 128
TAPS = 64
HALF = 32
KSIG = 16
CAP = 16
SIGD = 256
FIELDS = 16
SHIFTS = 16
DEPTH = 5 * 1024
GROUPS = 16
OWN_IDS = 512
CLIPS = 1024
LIB_DEV = 2048
SHARP = 400.0
F32 = jnp.float32
BF16 = jnp.bfloat16
I32 = jnp.int32
MESH = pl.DeviceIdType.MESH
HIGHEST = lax.Precision.HIGHEST

PLANE = sorted(
    [(dx, dy) for dx in range(4) for dy in range(4) if dx or dy],
    key=lambda d: -(min(d[0], 4 - d[0]) + min(d[1], 4 - d[1])),
)
LINE = sorted(
    [(dz, dc) for dz in range(8) for dc in range(2) if dz or dc],
    key=lambda d: -(2 * min(d[0], 8 - d[0]) + d[1]),
)
SAME_CORE = sorted(
    [(dx, dy, dz) for dx in range(4) for dy in range(4) for dz in range(8) if dx or dy or dz],
    key=lambda d: -(min(d[0], 4 - d[0]) + min(d[1], 4 - d[1]) + min(d[2], 8 - d[2])),
)
AROUND = [(1, 0), (-1, 0), (0, 1), (0, -1)]


def place():
    w = lax.axis_index("wide")
    n = lax.axis_index("narrow")
    return w, n


def plane_peer(w, n, d):
    g = w // 4
    x = (g // 4 + d[0]) % 4
    y = (g % 4 + d[1]) % 4
    return (x * 4 + y) * 4 + w % 4, n


def line_peer(w, n, d):
    z = (n * 2 + (w // 2) % 2 + d[0]) % 8
    c = (w % 2 + d[1]) % 2
    return (w // 4) * 4 + (z % 2) * 2 + c, z // 2


def around_peer(w, n, d):
    return (w + d[0] + 64) % 64, (n + d[1] + 4) % 4


def iota(shape, dim):
    return lax.broadcasted_iota(I32, shape, dim)


def dot(a, b, precision=None):
    return jnp.dot(a, b, preferred_element_type=F32, precision=precision)


def dot_nt(a, b, precision=None):
    return lax.dot_general(
        a, b, (((1,), (1,)), ((), ())), preferred_element_type=F32, precision=precision
    )


def wait_bytes(ref, sem):
    pltpu.make_async_copy(ref, ref, sem).wait()


def unit_rows(matrix):
    mean_square = jnp.mean(matrix * matrix, axis=1, keepdims=True)
    return (matrix / (KSIG * jnp.sqrt(mean_square + 1e-06))).astype(BF16)


def build_taps(kern_ref, raw_taps, perm, taps):
    for block in range(8):
        p = iota((128, 1024), 0) + block * 128
        q = iota((128, 1024), 1)
        hit = q == (p % 64) * 16 + p // 64
        perm[block * 128 : block * 128 + 128, :] = jnp.where(hit, 1.0, 0.0).astype(BF16)
    for i in range(0, TAPS, 2):
        pair = jnp.concatenate(
            [kern_ref[pl.ds(i, 16, stride=64), :], kern_ref[pl.ds(i + 1, 16, stride=64), :]],
            axis=1,
        )
        high = pair.astype(BF16)
        low = (pair - high.astype(F32)).astype(BF16)
        row = (i // 16) * 32
        lane = (i % 16) * 64
        raw_taps[row : row + 16, lane : lane + 128] = high
        raw_taps[row + 16 : row + 32, lane : lane + 128] = low
    raw_taps[...] = dot(raw_taps[...], perm[...]).astype(BF16)

    def shift(s, carry):
        inner = iota((32, 128), 1) % 16
        wrap = inner >= 16 - s
        row = pl.multiple_of(s * 16, 16)
        for v in range(8):
            lanes = slice(v * 128, v * 128 + 128)
            for ib in range(5):
                zero = jnp.zeros((32, 128), BF16)
                here = raw_taps[ib * 32 : ib * 32 + 32, lanes] if ib < 4 else zero
                if ib > 0:
                    last = pltpu.roll(raw_taps[ib * 32 - 32 : ib * 32, lanes], 112, 1)
                else:
                    last = zero
                moved = pltpu.roll(jnp.where(wrap, last, here), s, 1)
                to = slice(ib * 1024 + v * 128, ib * 1024 + v * 128 + 128)
                taps[pl.ds(row, 16), to] = moved[0:16]
                taps[pl.ds(row + 256, 16), to] = moved[16:32]
        return carry

    lax.fori_loop(0, SHIFTS, shift, 0)


def cosine(m):
    v = (64 - jnp.abs(m - 128)).astype(F32) * (math.pi / 128)
    s = v * v
    poly = 1.0 / 6227020800.0
    for c in (-1.0 / 39916800, 1.0 / 362880, -1.0 / 5040, 1.0 / 120, -1.0 / 6, 1.0):
        poly = poly * s + c
    return -(v * poly)


def shifted_basis(corner):
    spread = (iota((256, 16), 0) // 16 == iota((256, 16), 1)).astype(F32)
    corners = dot(spread, jnp.broadcast_to(corner, (16, 128))).astype(I32)
    k = iota((256, 128), 0) % 16
    offset = iota((256, 128), 1) - corners
    inside = (offset >= 0) & (offset < 64)
    weight = jnp.where(k == 0, math.sqrt(1.0 / 64), math.sqrt(2.0 / 64)).astype(F32)
    m = jnp.where(inside, ((2 * offset + 1) * k) % 256, 0)
    return jnp.where(inside, weight * cosine(m), 0.0)


def own_bases(w, n, tile_ref, corner_ref, row_basis, col_basis):
    owned = (tile_ref[...] == n * 64 + w).astype(F32)
    earlier = (iota((128, 128), 0) < iota((128, 128), 1)).astype(F32)
    before = dot(owned, earlier)
    base = jnp.zeros((1, 1), F32)
    slot = iota((16, 128), 0).astype(F32)
    rows = jnp.zeros((16, 128), F32)
    cols = jnp.zeros((16, 128), F32)
    for r in range(8):
        own = owned[r : r + 1]
        here = (own > 0) & (before[r : r + 1] + base == slot)
        part = slice(r * 128, r * 128 + 128)
        rows += jnp.where(here, corner_ref[0:1, part].astype(F32), 0.0)
        cols += jnp.where(here, corner_ref[1:2, part].astype(F32), 0.0)
        base += jnp.sum(own, axis=1, keepdims=True)
    row_basis[...] = shifted_basis(jnp.sum(rows, axis=1, keepdims=True))
    col_basis[...] = shifted_basis(jnp.sum(cols, axis=1, keepdims=True))


def build_select(w, tile_ref, select):
    core = w % 2
    q = iota((64, 256), 1)
    dev = q // 16
    slot_key = ((dev % 4) * 64 + (w // 4) * 4 + dev // 4) * 16 + q % 16
    for r in range(8):
        m = iota((64, 128), 0) + r * 64
        ids = (m // 16) * 32 + core * 16 + m % 16
        lane = iota((64, 128), 1)
        tiles = tile_ref[r : r + 1, :]
        mine = jnp.sum(
            jnp.where(ids == lane + r * 128, tiles.astype(F32), 0.0), axis=1, keepdims=True
        )
        rank = jnp.zeros((64, 128), F32)
        for b in range(r + 1):
            same = tile_ref[b : b + 1, :].astype(F32) == mine
            if b == r:
                same = same & (lane + r * 128 < ids)
            rank += jnp.where(same, 1.0, 0.0)
        key = (mine * 16.0 + jnp.sum(rank, axis=1, keepdims=True)).astype(I32)
        select[r * 64 : r * 64 + 64, :] = (key == slot_key).astype(F32).astype(BF16)


def shifted_copies(left, mid, right, places):
    lane = iota(mid.shape, 1)
    mid = pltpu.roll(mid, HALF, 1)
    low = jnp.where(lane < HALF, left, mid)
    high = jnp.where(lane < HALF, mid, right)
    for j in range(TAPS):
        moved = jnp.where(lane < j, high, low)
        if j:
            moved = pltpu.roll(moved, 128 - j, 1)
        for b, where in enumerate(places):
            for ref, index, at in where:
                row = index * 1024 + j * 16
                ref[row : row + 16, at : at + 128] = moved[b * 16 : b * 16 + 16]


def rolled(x, shift):
    return pltpu.roll(x, shift % 128, 1) if shift % 128 else x


def pack_side(mask, first):
    lane = iota((HALF, TILE), 1)
    packed = jnp.zeros((HALF, TILE), BF16)
    for q in range(4):
        moved = rolled(mask[q * 32 : q * 32 + 32, :], q * 32 - first)
        packed = jnp.where(lane // 32 == q, moved, packed)
    return packed


def kernel(
    raster_hbm, trans_hbm, kern_hbm, weight_hbm, lib_ref, tile_hbm, corner_hbm,
    aerial_ref, score_ref,
    raster_ref, trans_ref, kern_ref, weight_ref, tile_ref, corner_ref, in_sem,
    mask, packed, side, edge, corner, raw_taps, perm, taps, inner, outer, row_basis, col_basis, select,
    lib_raw, units, slots, parts, sums, clips, turned, own_lse, all_lse,
    halo_send, halo_recv, corner_send, corner_recv, lib_sem, pair_send, pair_recv,
    line_send, line_recv, sum_send, sum_recv, all_send, all_recv,
    lse_send, lse_recv,
):
    w, n = place()
    g = w // 4
    core = w % 2
    line_me = (w % 4) * 4 + n
    me = g * 8 + n * 2 + (w // 2) % 2
    around = [around_peer(w, n, d) for d in AROUND]
    line = [line_peer(w, n, d) for d in LINE]
    plane = [plane_peer(w, n, d) for d in PLANE]

    barrier = pltpu.get_barrier_semaphore()
    peers = around + line + plane
    for peer in peers:
        pl.semaphore_signal(barrier, inc=1, device_id=peer, device_id_type=MESH)
    inputs = [
        pltpu.make_async_copy(src, dst, in_sem.at[i])
        for i, (src, dst) in enumerate([
            (raster_hbm, raster_ref), (trans_hbm, trans_ref), (kern_hbm, kern_ref),
            (weight_hbm, weight_ref), (tile_hbm, tile_ref), (corner_hbm, corner_ref),
        ])
    ]
    for copy in inputs:
        copy.start()
    lib_copy = pltpu.make_async_copy(lib_ref, lib_raw, lib_sem)
    lib_copy.start()
    for copy in inputs:
        copy.wait()
    mask[...] = (raster_ref[...].astype(F32) * trans_ref[...].astype(F32)).astype(BF16)
    packed[0] = pack_side(mask[...], 0)
    packed[1] = pack_side(mask[...], 96)
    build_taps(kern_ref, raw_taps, perm, taps)
    pl.semaphore_wait(barrier, len(peers))

    def send(src, dst, ssem, rsem, peer):
        copy = pltpu.make_async_remote_copy(
            src_ref=src, dst_ref=dst, send_sem=ssem, recv_sem=rsem,
            device_id=peer, device_id_type=MESH,
        )
        copy.start()
        return copy

    halo = []
    pieces = [(packed.at[1], side.at[0]), (packed.at[0], side.at[1]), (mask.at[96:128], edge.at[0]), (mask.at[0:32], edge.at[1])]
    for i, (src, dst) in enumerate(pieces):
        halo.append(send(src, dst, halo_send.at[i], halo_recv.at[i], around[i]))

    lib_copy.wait()

    def normal(i, carry):
        at = pl.ds(pl.multiple_of(i * 256, 256), 256)
        units[0, at, :] = unit_rows(lib_raw[at, :].astype(F32))
        return carry

    lax.fori_loop(0, LIB_DEV // 256, normal, 0)
    other = line_peer(w, n, (0, 1))
    pair = send(units.at[0], units.at[1], pair_send, pair_recv, other)
    own_bases(w, n, tile_ref, corner_ref, row_basis, col_basis)
    build_select(w, tile_ref, select)

    for copy in halo[:2]:
        copy.wait()

    @pl.when(w == 0)
    def _():
        side[0] = jnp.zeros((HALF, TILE), BF16)

    @pl.when(w == 63)
    def _():
        side[1] = jnp.zeros((HALF, TILE), BF16)

    below, above = around[2], around[3]
    pieces = [(side, corner.at[0], below), (side, corner.at[1], above)]
    corners = []
    for i, (src, dst, peer) in enumerate(pieces):
        corners.append(send(src, dst, corner_send.at[i], corner_recv.at[i], peer))

    places = [[] for _ in range(8)]
    for b in range(8):
        rb = b + 2
        if rb < 8:
            places[b].append((inner, rb - 2, 0))
        if rb >= 4:
            places[b].append((inner, rb - 4, 128))
        places[b].append((outer, rb, 0) if rb < 6 else (outer, rb - 6, 128))
    lefts = jnp.concatenate([rolled(side[0], -32 * q) for q in range(4)], axis=0)
    rights = jnp.concatenate([rolled(side[1], 32 - 32 * q) for q in range(4)], axis=0)
    shifted_copies(lefts, mask[...], rights, places)

    field_index = iota((16, 256), 0) // 2
    weight = jnp.zeros((16, 256), F32)
    for k in range(8):
        weight = jnp.where(field_index == k, weight_ref[k], weight)

    def rows(source, first, second):
        def pair_of_blocks(i):
            window = source[i * 1024 : i * 1024 + DEPTH, :]
            both = dot(taps[...], window)
            field = both[0:256] + both[256:512]
            energy = (field * field).reshape(SHIFTS, FIELDS, 256) * weight[None]
            image = jnp.sum(energy, axis=1)
            for lane, block in ((0, first + i), (128, second + i)):
                aerial_ref[block * 16 : block * 16 + 16, :] = image[:, lane : lane + 128]

        for i in range(2):
            pair_of_blocks(i)

    rows(inner, 2, 4)
    for copy in halo[2:] + corners:
        copy.wait()

    @pl.when(n == 0)
    def _():
        edge[0] = jnp.zeros((HALF, TILE), BF16)
        corner[0] = jnp.zeros((2, HALF, TILE), BF16)

    @pl.when(n == 3)
    def _():
        edge[1] = jnp.zeros((HALF, TILE), BF16)
        corner[1] = jnp.zeros((2, HALF, TILE), BF16)

    places = [[(outer, 0, 0)], [(outer, 1, 0)], [(outer, 4, 128)], [(outer, 5, 128)]]
    shifted_copies(
        jnp.concatenate([rolled(corner[0, 0], -96), corner[1, 0]], axis=0),
        edge[...].reshape(2 * HALF, TILE),
        jnp.concatenate([rolled(corner[0, 1], -64), rolled(corner[1, 1], 32)], axis=0),
        places,
    )
    rows(outer, 0, 6)

    halfway = dot(row_basis[...], aerial_ref[...], HIGHEST)
    cross = dot_nt(halfway, col_basis[...], HIGHEST)
    row = iota((256, 256), 0)
    lane = iota((256, 256), 1)
    cross = jnp.where(row // 16 == lane // 16, cross, 0.0)
    fold = (row % 16 == lane % 16).astype(F32)
    wide = jnp.where(row % 16 == lane // 16, dot(cross, fold, HIGHEST), 0.0)
    signature = jnp.sum(wide.reshape(CAP, KSIG, SIGD), axis=1)
    signature = jnp.where(iota((CAP, SIGD), 1) == 0, 0.0, signature)
    slots[line_me] = unit_rows(signature)

    for peer in line:
        send(slots.at[line_me], slots.at[line_me], line_send, line_recv, peer)
    wait_bytes(slots.at[0:15], line_recv)
    picked = dot(select[...], slots[...].reshape(256, SIGD)).astype(BF16)
    parts[...] = picked.reshape(GROUPS, 32, SIGD)

    for i, d in enumerate(PLANE):
        gp = plane[i][0] // 4
        send(parts.at[gp], sums.at[g], sum_send, sum_recv, plane[i])
    sums[g] = parts[g]
    wait_bytes(sums.at[0:15], sum_recv)
    total = sums[0].astype(F32)
    for i in range(1, GROUPS):
        total += sums[i].astype(F32)
    clips[g] = total.astype(BF16)

    for peer in plane:
        send(clips.at[g], clips.at[g], all_send, all_recv, peer)
    pair.wait()
    wait_bytes(clips.at[0:15], all_recv)

    scale = SHARP * math.log2(math.e)
    turned[...] = jnp.transpose(clips[...].reshape(OWN_IDS, SIGD))
    tops = jnp.full((8, OWN_IDS), -4.0, F32)
    sums_of = jnp.zeros((8, OWN_IDS), F32)
    for block in range(2 * LIB_DEV // 512):
        at = (block % 4) * 512
        near = dot(units[block // 4, at : at + 512, :], turned[...]).reshape(64, 8, OWN_IDS)
        old = tops
        tops = jnp.maximum(old, jnp.max(near, axis=0))
        gain = jnp.sum(jnp.exp2((near - tops[None]) * scale), axis=0)
        sums_of = sums_of * jnp.exp2((old - tops) * scale) + gain
    top = jnp.max(tops, axis=0, keepdims=True)
    amount = jnp.sum(sums_of * jnp.exp2((tops - top) * scale), axis=0, keepdims=True)
    found = (top - 1.0) * SHARP + jnp.log(amount)
    for block in range(4):
        own_lse[block] = found[:, block * 128 : block * 128 + 128]

    columns = {(0, 0): g} | {d: plane[i][0] // 4 for i, d in enumerate(PLANE)}
    quarters = {d: c // 4 for d, c in columns.items()}
    starts = {d: c * 4 for d, c in columns.items()}
    rows_z = {d: line_peer(w, n, (d, 0)) for d in range(8)}
    within = {d: p[0] % 4 for d, p in rows_z.items()}
    for dx, dy, dz in SAME_CORE:
        peer = (starts[dx, dy] + within[dz], rows_z[dz][1])
        send(own_lse.at[quarters[dx, dy]], all_lse.at[me], lse_send, lse_recv, peer)
    all_lse[me] = own_lse[g // 4]
    wait_bytes(all_lse.at[0:127], lse_recv)
    every = all_lse[...]
    top = jnp.max(every, axis=0)
    score = (top + jnp.log(jnp.sum(jnp.exp(every - top[None]), axis=0))) / (-SHARP)
    first = (g % 4) * 32 + ((w // 2) % 2) * 16 + n * 4
    spot = iota((1, 128), 1)
    for t in range(4):
        score_ref[t] = jnp.sum(jnp.where(spot == first + t, score, 0.0))

    wait_bytes(slots.at[0:15], line_send)
    wait_bytes(sums.at[0:15], sum_send)
    wait_bytes(clips.at[0:15], all_send)
    wait_bytes(all_lse.at[0:127], lse_send)


def per_device(raster, transmission, kernels, kernel_weight, library, clip_tile, clip_corner):
    hbm = pl.BlockSpec(memory_space=pl.ANY)
    smem = pl.BlockSpec(memory_space=pltpu.SMEM)
    dma = pltpu.SemaphoreType.DMA
    return pl.pallas_call(
        kernel,
        out_shape=(pltpu.VMEM((TILE, TILE), F32), jax.ShapeDtypeStruct((4,), F32)),
        in_specs=[hbm] * 7,
        out_specs=(pl.BlockSpec(memory_space=pltpu.VMEM), smem),
        scratch_shapes=[
            pltpu.VMEM((TILE, TILE), I32),
            pltpu.VMEM((TILE, TILE), BF16),
            pltpu.VMEM((FIELDS * TAPS, TAPS), F32),
            pltpu.SMEM((8,), F32),
            pltpu.VMEM((8, 128), I32),
            pltpu.VMEM((2, CLIPS), I32),
            dma((6,)),
            pltpu.VMEM((TILE, TILE), BF16),
            pltpu.VMEM((2, HALF, TILE), BF16),
            pltpu.VMEM((2, HALF, TILE), BF16),
            pltpu.VMEM((2, HALF, TILE), BF16),
            pltpu.VMEM((2, 2, HALF, TILE), BF16),
            pltpu.VMEM((128, 1024), BF16),
            pltpu.VMEM((1024, 1024), BF16),
            pltpu.VMEM((512, DEPTH), BF16),
            pltpu.VMEM((6 * 1024, 256), BF16),
            pltpu.VMEM((6 * 1024, 256), BF16),
            pltpu.VMEM((256, TILE), F32),
            pltpu.VMEM((256, TILE), F32),
            pltpu.VMEM((OWN_IDS, 256), BF16),
            pltpu.VMEM((LIB_DEV, SIGD), BF16),
            pltpu.VMEM((2, LIB_DEV, SIGD), BF16),
            pltpu.VMEM((16, CAP, SIGD), BF16),
            pltpu.VMEM((GROUPS, 32, SIGD), BF16),
            pltpu.VMEM((GROUPS, 32, SIGD), BF16),
            pltpu.VMEM((GROUPS, 32, SIGD), BF16),
            pltpu.VMEM((SIGD, OWN_IDS), BF16),
            pltpu.VMEM((4, 1, 128), F32),
            pltpu.VMEM((128, 1, 128), F32),
            dma((4,)), dma((4,)), dma((2,)), dma((2,)), dma, dma, dma,
            dma, dma, dma, dma, dma, dma, dma, dma,
        ],
        compiler_params=pltpu.CompilerParams(
            collective_id=0, has_side_effects=True, vmem_limit_bytes=56 * 1024 * 1024
        ),
    )(
        raster,
        transmission,
        kernels.reshape(FIELDS * TAPS, TAPS),
        kernel_weight,
        library,
        clip_tile.reshape(8, 128),
        clip_corner,
    )


def solution(mesh):
    placed = (
        P("narrow", "wide"),
        P("narrow", "wide"),
        P(),
        P(),
        P(("wide", "narrow"), None),
        P(),
        P(),
    )
    return jax.shard_map(
        per_device,
        mesh=mesh,
        in_specs=placed,
        out_specs=(P("narrow", "wide"), P(("wide", "narrow"))),
        check_vma=False,
    )
```

```python
import math

import jax
import jax.numpy as jnp
from jax import lax
from jax.experimental import pallas as pl
from jax.experimental.pallas import tpu as pltpu
from jax.sharding import PartitionSpec as P

TILE = 128
TAPS = 64
HALF = 32
KSIG = 16
CAP = 16
SIGD = 256
FIELDS = 16
SHIFTS = 16
DEPTH = 5 * 1024
GROUPS = 16
OWN_IDS = 512
CLIPS = 1024
LIB_DEV = 2048
SHARP = 400.0
F32 = jnp.float32
BF16 = jnp.bfloat16
I32 = jnp.int32
MESH = pl.DeviceIdType.MESH
HIGHEST = lax.Precision.HIGHEST

PLANE = sorted(
    [(dx, dy) for dx in range(4) for dy in range(4) if dx or dy],
    key=lambda d: -(min(d[0], 4 - d[0]) + min(d[1], 4 - d[1])),
)
LINE = sorted(
    [(dz, dc) for dz in range(8) for dc in range(2) if dz or dc],
    key=lambda d: -(2 * min(d[0], 8 - d[0]) + d[1]),
)
SAME_CORE = sorted(
    [(dx, dy, dz) for dx in range(4) for dy in range(4) for dz in range(8) if dx or dy or dz],
    key=lambda d: -(min(d[0], 4 - d[0]) + min(d[1], 4 - d[1]) + min(d[2], 8 - d[2])),
)
AROUND = [(1, 0), (-1, 0), (0, 1), (0, -1)]


def place():
    w = lax.axis_index("wide")
    n = lax.axis_index("narrow")
    return w, n


def plane_peer(w, n, d):
    g = w // 4
    x = (g // 4 + d[0]) % 4
    y = (g % 4 + d[1]) % 4
    return (x * 4 + y) * 4 + w % 4, n


def line_peer(w, n, d):
    z = (n * 2 + (w // 2) % 2 + d[0]) % 8
    c = (w % 2 + d[1]) % 2
    return (w // 4) * 4 + (z % 2) * 2 + c, z // 2


def around_peer(w, n, d):
    return (w + d[0] + 64) % 64, (n + d[1] + 4) % 4


def iota(shape, dim):
    return lax.broadcasted_iota(I32, shape, dim)


def dot(a, b, precision=None):
    return jnp.dot(a, b, preferred_element_type=F32, precision=precision)


def dot_nt(a, b, precision=None):
    return lax.dot_general(
        a, b, (((1,), (1,)), ((), ())), preferred_element_type=F32, precision=precision
    )


def wait_bytes(ref, sem):
    pltpu.make_async_copy(ref, ref, sem).wait()


def unit_rows(matrix):
    mean_square = jnp.mean(matrix * matrix, axis=1, keepdims=True)
    return (matrix / (KSIG * jnp.sqrt(mean_square + 1e-06))).astype(BF16)


def build_taps(kern_ref, raw_taps, perm, taps):
    for block in range(8):
        p = iota((128, 1024), 0) + block * 128
        q = iota((128, 1024), 1)
        hit = q == (p % 64) * 16 + p // 64
        perm[block * 128 : block * 128 + 128, :] = jnp.where(hit, 1.0, 0.0).astype(BF16)
    for i in range(0, TAPS, 2):
        pair = jnp.concatenate(
            [kern_ref[pl.ds(i, 16, stride=64), :], kern_ref[pl.ds(i + 1, 16, stride=64), :]],
            axis=1,
        )
        high = pair.astype(BF16)
        low = (pair - high.astype(F32)).astype(BF16)
        row = (i // 16) * 32
        lane = (i % 16) * 64
        raw_taps[row : row + 16, lane : lane + 128] = high
        raw_taps[row + 16 : row + 32, lane : lane + 128] = low
    raw_taps[...] = dot(raw_taps[...], perm[...]).astype(BF16)

    def shift(s, carry):
        inner = iota((32, 128), 1) % 16
        wrap = inner >= 16 - s
        row = pl.multiple_of(s * 16, 16)
        for v in range(8):
            lanes = slice(v * 128, v * 128 + 128)
            for ib in range(5):
                zero = jnp.zeros((32, 128), BF16)
                here = raw_taps[ib * 32 : ib * 32 + 32, lanes] if ib < 4 else zero
                if ib > 0:
                    last = pltpu.roll(raw_taps[ib * 32 - 32 : ib * 32, lanes], 112, 1)
                else:
                    last = zero
                moved = pltpu.roll(jnp.where(wrap, last, here), s, 1)
                to = slice(ib * 1024 + v * 128, ib * 1024 + v * 128 + 128)
                taps[pl.ds(row, 16), to] = moved[0:16]
                taps[pl.ds(row + 256, 16), to] = moved[16:32]
        return carry

    lax.fori_loop(0, SHIFTS, shift, 0)


def cosine(m):
    v = (64 - jnp.abs(m - 128)).astype(F32) * (math.pi / 128)
    s = v * v
    poly = 1.0 / 6227020800.0
    for c in (-1.0 / 39916800, 1.0 / 362880, -1.0 / 5040, 1.0 / 120, -1.0 / 6, 1.0):
        poly = poly * s + c
    return -(v * poly)


def shifted_basis(corner):
    spread = (iota((256, 16), 0) // 16 == iota((256, 16), 1)).astype(F32)
    corners = dot(spread, jnp.broadcast_to(corner, (16, 128))).astype(I32)
    k = iota((256, 128), 0) % 16
    offset = iota((256, 128), 1) - corners
    inside = (offset >= 0) & (offset < 64)
    weight = jnp.where(k == 0, math.sqrt(1.0 / 64), math.sqrt(2.0 / 64)).astype(F32)
    m = jnp.where(inside, ((2 * offset + 1) * k) % 256, 0)
    return jnp.where(inside, weight * cosine(m), 0.0)


def own_bases(w, n, tile_ref, corner_ref, row_basis, col_basis):
    owned = (tile_ref[...] == n * 64 + w).astype(F32)
    earlier = (iota((128, 128), 0) < iota((128, 128), 1)).astype(F32)
    before = dot(owned, earlier)
    base = jnp.zeros((1, 1), F32)
    slot = iota((16, 128), 0).astype(F32)
    rows = jnp.zeros((16, 128), F32)
    cols = jnp.zeros((16, 128), F32)
    for r in range(8):
        own = owned[r : r + 1]
        here = (own > 0) & (before[r : r + 1] + base == slot)
        part = slice(r * 128, r * 128 + 128)
        rows += jnp.where(here, corner_ref[0:1, part].astype(F32), 0.0)
        cols += jnp.where(here, corner_ref[1:2, part].astype(F32), 0.0)
        base += jnp.sum(own, axis=1, keepdims=True)
    row_basis[...] = shifted_basis(jnp.sum(rows, axis=1, keepdims=True))
    col_basis[...] = shifted_basis(jnp.sum(cols, axis=1, keepdims=True))


def build_select(w, tile_ref, select):
    core = w % 2
    q = iota((64, 256), 1)
    dev = q // 16
    slot_key = ((dev % 4) * 64 + (w // 4) * 4 + dev // 4) * 16 + q % 16
    for r in range(8):
        m = iota((64, 128), 0) + r * 64
        ids = (m // 16) * 32 + core * 16 + m % 16
        lane = iota((64, 128), 1)
        tiles = tile_ref[r : r + 1, :]
        mine = jnp.sum(
            jnp.where(ids == lane + r * 128, tiles.astype(F32), 0.0), axis=1, keepdims=True
        )
        rank = jnp.zeros((64, 128), F32)
        for b in range(r + 1):
            same = tile_ref[b : b + 1, :].astype(F32) == mine
            if b == r:
                same = same & (lane + r * 128 < ids)
            rank += jnp.where(same, 1.0, 0.0)
        key = (mine * 16.0 + jnp.sum(rank, axis=1, keepdims=True)).astype(I32)
        select[r * 64 : r * 64 + 64, :] = (key == slot_key).astype(F32).astype(BF16)


def shifted_copies(left, mid, right, places):
    lane = iota(mid.shape, 1)
    mid = pltpu.roll(mid, HALF, 1)
    low = jnp.where(lane < HALF, left, mid)
    high = jnp.where(lane < HALF, mid, right)
    for j in range(TAPS):
        moved = jnp.where(lane < j, high, low)
        if j:
            moved = pltpu.roll(moved, 128 - j, 1)
        for b, where in enumerate(places):
            for ref, index, at in where:
                row = index * 1024 + j * 16
                ref[row : row + 16, at : at + 128] = moved[b * 16 : b * 16 + 16]


def rolled(x, shift):
    return pltpu.roll(x, shift % 128, 1) if shift % 128 else x


def pack_side(mask, first):
    lane = iota((HALF, TILE), 1)
    packed = jnp.zeros((HALF, TILE), BF16)
    for q in range(4):
        moved = rolled(mask[q * 32 : q * 32 + 32, :], q * 32 - first)
        packed = jnp.where(lane // 32 == q, moved, packed)
    return packed


def kernel(
    raster_hbm, trans_hbm, kern_hbm, weight_hbm, lib_ref, tile_hbm, corner_hbm,
    aerial_ref, score_ref,
    raster_ref, trans_ref, kern_ref, weight_ref, tile_ref, corner_ref, in_sem,
    mask, packed, side, edge, corner, raw_taps, perm, taps, inner, outer, row_basis, col_basis, select,
    lib_raw, units, slots, parts, sums, clips, turned, own_lse, all_lse,
    halo_send, halo_recv, corner_send, corner_recv, lib_sem, pair_send, pair_recv,
    line_send, line_recv, sum_send, sum_recv, all_send, all_recv,
    lse_send, lse_recv,
):
    w, n = place()
    g = w // 4
    core = w % 2
    line_me = (w % 4) * 4 + n
    me = g * 8 + n * 2 + (w // 2) % 2
    around = [around_peer(w, n, d) for d in AROUND]
    line = [line_peer(w, n, d) for d in LINE]
    plane = [plane_peer(w, n, d) for d in PLANE]

    barrier = pltpu.get_barrier_semaphore()
    peers = around + line + plane
    for peer in peers:
        pl.semaphore_signal(barrier, inc=1, device_id=peer, device_id_type=MESH)
    inputs = [
        pltpu.make_async_copy(src, dst, in_sem.at[i])
        for i, (src, dst) in enumerate([
            (raster_hbm, raster_ref), (trans_hbm, trans_ref), (kern_hbm, kern_ref),
            (weight_hbm, weight_ref), (tile_hbm, tile_ref), (corner_hbm, corner_ref),
        ])
    ]
    for copy in inputs:
        copy.start()
    lib_copy = pltpu.make_async_copy(lib_ref, lib_raw, lib_sem)
    lib_copy.start()
    for copy in inputs:
        copy.wait()
    mask[...] = (raster_ref[...].astype(F32) * trans_ref[...].astype(F32)).astype(BF16)
    packed[0] = pack_side(mask[...], 0)
    packed[1] = pack_side(mask[...], 96)
    build_taps(kern_ref, raw_taps, perm, taps)
    pl.semaphore_wait(barrier, len(peers))

    def send(src, dst, ssem, rsem, peer):
        copy = pltpu.make_async_remote_copy(
            src_ref=src, dst_ref=dst, send_sem=ssem, recv_sem=rsem,
            device_id=peer, device_id_type=MESH,
        )
        copy.start()
        return copy

    halo = []
    pieces = [(packed.at[1], side.at[0]), (packed.at[0], side.at[1]), (mask.at[96:128], edge.at[0]), (mask.at[0:32], edge.at[1])]
    for i, (src, dst) in enumerate(pieces):
        halo.append(send(src, dst, halo_send.at[i], halo_recv.at[i], around[i]))

    lib_copy.wait()

    def normal(i, carry):
        at = pl.ds(pl.multiple_of(i * 256, 256), 256)
        units[0, at, :] = unit_rows(lib_raw[at, :].astype(F32))
        return carry

    lax.fori_loop(0, LIB_DEV // 256, normal, 0)
    other = line_peer(w, n, (0, 1))
    pair = send(units.at[0], units.at[1], pair_send, pair_recv, other)
    own_bases(w, n, tile_ref, corner_ref, row_basis, col_basis)
    build_select(w, tile_ref, select)

    for copy in halo[:2]:
        copy.wait()

    @pl.when(w == 0)
    def _():
        side[0] = jnp.zeros((HALF, TILE), BF16)

    @pl.when(w == 63)
    def _():
        side[1] = jnp.zeros((HALF, TILE), BF16)

    below, above = around[2], around[3]
    pieces = [(side, corner.at[0], below), (side, corner.at[1], above)]
    corners = []
    for i, (src, dst, peer) in enumerate(pieces):
        corners.append(send(src, dst, corner_send.at[i], corner_recv.at[i], peer))

    places = [[] for _ in range(8)]
    for b in range(8):
        rb = b + 2
        if rb < 8:
            places[b].append((inner, rb - 2, 0))
        if rb >= 4:
            places[b].append((inner, rb - 4, 128))
        places[b].append((outer, rb, 0) if rb < 6 else (outer, rb - 6, 128))
    lefts = jnp.concatenate([rolled(side[0], -32 * q) for q in range(4)], axis=0)
    rights = jnp.concatenate([rolled(side[1], 32 - 32 * q) for q in range(4)], axis=0)
    shifted_copies(lefts, mask[...], rights, places)

    field_index = iota((16, 256), 0) // 2
    weight = jnp.zeros((16, 256), F32)
    for k in range(8):
        weight = jnp.where(field_index == k, weight_ref[k], weight)

    def rows(source, first, second):
        def pair_of_blocks(i):
            window = source[i * 1024 : i * 1024 + DEPTH, :]
            both = dot(taps[...], window)
            field = both[0:256] + both[256:512]
            energy = (field * field).reshape(SHIFTS, FIELDS, 256) * weight[None]
            image = jnp.sum(energy, axis=1)
            for lane, block in ((0, first + i), (128, second + i)):
                aerial_ref[block * 16 : block * 16 + 16, :] = image[:, lane : lane + 128]

        for i in range(2):
            pair_of_blocks(i)

    rows(inner, 2, 4)
    for copy in halo[2:] + corners:
        copy.wait()

    @pl.when(n == 0)
    def _():
        edge[0] = jnp.zeros((HALF, TILE), BF16)
        corner[0] = jnp.zeros((2, HALF, TILE), BF16)

    @pl.when(n == 3)
    def _():
        edge[1] = jnp.zeros((HALF, TILE), BF16)
        corner[1] = jnp.zeros((2, HALF, TILE), BF16)

    places = [[(outer, 0, 0)], [(outer, 1, 0)], [(outer, 4, 128)], [(outer, 5, 128)]]
    shifted_copies(
        jnp.concatenate([rolled(corner[0, 0], -96), corner[1, 0]], axis=0),
        edge[...].reshape(2 * HALF, TILE),
        jnp.concatenate([rolled(corner[0, 1], -64), rolled(corner[1, 1], 32)], axis=0),
        places,
    )
    rows(outer, 0, 6)

    halfway = dot(row_basis[...], aerial_ref[...], HIGHEST)
    cross = dot_nt(halfway, col_basis[...], HIGHEST)
    row = iota((256, 256), 0)
    lane = iota((256, 256), 1)
    cross = jnp.where(row // 16 == lane // 16, cross, 0.0)
    folded = cross[:, 0:128] + cross[:, 128:256]
    for shift in (64, 32, 16):
        folded = folded + pltpu.roll(folded, shift, 1)
    folded = jnp.concatenate([folded, folded], axis=1)
    wide = jnp.where(row % 16 == lane // 16, folded, 0.0)
    signature = jnp.sum(wide.reshape(CAP, KSIG, SIGD), axis=1)
    signature = jnp.where(iota((CAP, SIGD), 1) == 0, 0.0, signature)
    slots[line_me] = unit_rows(signature)

    for peer in line:
        send(slots.at[line_me], slots.at[line_me], line_send, line_recv, peer)
    wait_bytes(slots.at[0:15], line_recv)
    picked = dot(select[...], slots[...].reshape(256, SIGD)).astype(BF16)
    parts[...] = picked.reshape(GROUPS, 32, SIGD)

    for i, d in enumerate(PLANE):
        gp = plane[i][0] // 4
        send(parts.at[gp], sums.at[g], sum_send, sum_recv, plane[i])
    sums[g] = parts[g]
    wait_bytes(sums.at[0:15], sum_recv)
    total = sums[0].astype(F32)
    for i in range(1, GROUPS):
        total += sums[i].astype(F32)
    clips[g] = total.astype(BF16)

    for peer in plane:
        send(clips.at[g], clips.at[g], all_send, all_recv, peer)
    pair.wait()
    wait_bytes(clips.at[0:15], all_recv)

    scale = SHARP * math.log2(math.e)
    turned[...] = jnp.transpose(clips[...].reshape(OWN_IDS, SIGD))
    tops = jnp.full((8, OWN_IDS), -4.0, F32)
    sums_of = jnp.zeros((8, OWN_IDS), F32)
    for block in range(2 * LIB_DEV // 512):
        at = (block % 4) * 512
        near = dot(units[block // 4, at : at + 512, :], turned[...]).reshape(64, 8, OWN_IDS)
        old = tops
        tops = jnp.maximum(old, jnp.max(near, axis=0))
        gain = jnp.sum(jnp.exp2((near - tops[None]) * scale), axis=0)
        sums_of = sums_of * jnp.exp2((old - tops) * scale) + gain
    top = jnp.max(tops, axis=0, keepdims=True)
    amount = jnp.sum(sums_of * jnp.exp2((tops - top) * scale), axis=0, keepdims=True)
    found = (top - 1.0) * SHARP + jnp.log(amount)
    for block in range(4):
        own_lse[block] = found[:, block * 128 : block * 128 + 128]

    columns = {(0, 0): g} | {d: plane[i][0] // 4 for i, d in enumerate(PLANE)}
    quarters = {d: c // 4 for d, c in columns.items()}
    starts = {d: c * 4 for d, c in columns.items()}
    rows_z = {d: line_peer(w, n, (d, 0)) for d in range(8)}
    within = {d: p[0] % 4 for d, p in rows_z.items()}
    for dx, dy, dz in SAME_CORE:
        peer = (starts[dx, dy] + within[dz], rows_z[dz][1])
        send(own_lse.at[quarters[dx, dy]], all_lse.at[me], lse_send, lse_recv, peer)
    all_lse[me] = own_lse[g // 4]
    wait_bytes(all_lse.at[0:127], lse_recv)
    every = all_lse[...]
    top = jnp.max(every, axis=0)
    score = (top + jnp.log(jnp.sum(jnp.exp(every - top[None]), axis=0))) / (-SHARP)
    first = (g % 4) * 32 + ((w // 2) % 2) * 16 + n * 4
    spot = iota((1, 128), 1)
    for t in range(4):
        score_ref[t] = jnp.sum(jnp.where(spot == first + t, score, 0.0))

    wait_bytes(slots.at[0:15], line_send)
    wait_bytes(sums.at[0:15], sum_send)
    wait_bytes(clips.at[0:15], all_send)
    wait_bytes(all_lse.at[0:127], lse_send)


def per_device(raster, transmission, kernels, kernel_weight, library, clip_tile, clip_corner):
    hbm = pl.BlockSpec(memory_space=pl.ANY)
    smem = pl.BlockSpec(memory_space=pltpu.SMEM)
    dma = pltpu.SemaphoreType.DMA
    return pl.pallas_call(
        kernel,
        out_shape=(pltpu.VMEM((TILE, TILE), F32), jax.ShapeDtypeStruct((4,), F32)),
        in_specs=[hbm] * 7,
        out_specs=(pl.BlockSpec(memory_space=pltpu.VMEM), smem),
        scratch_shapes=[
            pltpu.VMEM((TILE, TILE), I32),
            pltpu.VMEM((TILE, TILE), BF16),
            pltpu.VMEM((FIELDS * TAPS, TAPS), F32),
            pltpu.SMEM((8,), F32),
            pltpu.VMEM((8, 128), I32),
            pltpu.VMEM((2, CLIPS), I32),
            dma((6,)),
            pltpu.VMEM((TILE, TILE), BF16),
            pltpu.VMEM((2, HALF, TILE), BF16),
            pltpu.VMEM((2, HALF, TILE), BF16),
            pltpu.VMEM((2, HALF, TILE), BF16),
            pltpu.VMEM((2, 2, HALF, TILE), BF16),
            pltpu.VMEM((128, 1024), BF16),
            pltpu.VMEM((1024, 1024), BF16),
            pltpu.VMEM((512, DEPTH), BF16),
            pltpu.VMEM((6 * 1024, 256), BF16),
            pltpu.VMEM((6 * 1024, 256), BF16),
            pltpu.VMEM((256, TILE), F32),
            pltpu.VMEM((256, TILE), F32),
            pltpu.VMEM((OWN_IDS, 256), BF16),
            pltpu.VMEM((LIB_DEV, SIGD), BF16),
            pltpu.VMEM((2, LIB_DEV, SIGD), BF16),
            pltpu.VMEM((16, CAP, SIGD), BF16),
            pltpu.VMEM((GROUPS, 32, SIGD), BF16),
            pltpu.VMEM((GROUPS, 32, SIGD), BF16),
            pltpu.VMEM((GROUPS, 32, SIGD), BF16),
            pltpu.VMEM((SIGD, OWN_IDS), BF16),
            pltpu.VMEM((4, 1, 128), F32),
            pltpu.VMEM((128, 1, 128), F32),
            dma((4,)), dma((4,)), dma((2,)), dma((2,)), dma, dma, dma,
            dma, dma, dma, dma, dma, dma, dma, dma,
        ],
        compiler_params=pltpu.CompilerParams(
            collective_id=0, has_side_effects=True, vmem_limit_bytes=56 * 1024 * 1024
        ),
    )(
        raster,
        transmission,
        kernels.reshape(FIELDS * TAPS, TAPS),
        kernel_weight,
        library,
        clip_tile.reshape(8, 128),
        clip_corner,
    )


def solution(mesh):
    placed = (
        P("narrow", "wide"),
        P("narrow", "wide"),
        P(),
        P(),
        P(("wide", "narrow"), None),
        P(),
        P(),
    )
    return jax.shard_map(
        per_device,
        mesh=mesh,
        in_specs=placed,
        out_specs=(P("narrow", "wide"), P(("wide", "narrow"))),
        check_vma=False,
    )
```
